128 devices in a mesh: ccd: 16 (over y, x), strip: 8 (over z, core).
Axes of the slice: x: 4, y: 4, z: 4, core: 2. Of those that a mesh axis runs over, the one named last changes fastest.
Arguments:
- images: bfloat16 [128, 256, 4096], P('ccd', 'strip'), may hold values from -6 to 6
- variances: bfloat16 [128, 256, 4096], P('ccd', 'strip'), may hold values from 0.25 to 4
- row_warp: bfloat16 [128, 256, 38], P('ccd', 'strip'), may hold values from -0.2 to 1, as said below
- col_warp: bfloat16 [2, 32, 384, 128], replicated, may hold values from -0.2 to 1, as said below
- warp_index: int32 [128, 8], P('ccd', 'strip'), may hold values from 0 to 1
- psf_kernels: bfloat16 [128, 3, 21], P('ccd'), may hold values from -1.1953125 to 1.1953125
- psf_coeff: float32 [128, 8, 3, 4096], P('ccd', 'strip'), may hold values from -3 to 3
- send_patch: int32 [128, 2], P('ccd'), may hold values from 0 to 15, all different within a row; in each aligned block of 8 rows (0 to 7, 8 to 15, ...) at most 2 rows name the same one
- send_offset: int32 [128, 2], P('ccd'), may hold values from 0 to 31
- request_patch: int32 [128, 2], P('ccd'), may hold values from 0 to 15, all different within a row; in each aligned block of 8 rows (0 to 7, 8 to 15, ...) at most 2 rows name the same one
- request_offset: int32 [128, 2], P('ccd'), may hold values from 0 to 31
- new_images: bfloat16 [128, 256, 4096], P('ccd', 'strip'), may hold values from -6 to 6
Outputs:
- patch_coadd: bfloat16 [16, 256, 4096], P('ccd', 'strip')
- difference: bfloat16 [128, 256, 4096], P('ccd', 'strip')
The draws below stay inside these ranges and needn't reach their ends.
Inputs may be any that keep to these rules, and one draw needn't show every extreme that they name: `row_warp`: each output row has its centre weight, 0.7 to 1.0, at its own row and side weights within -0.2 to 0.2 at the three rows on each side of it; all other entries are zero. `col_warp`: each output column has its centre weight, 0.7 to 1.0, at its own column and side weights within -0.2 to 0.2 at the three columns on each side of it; all other entries are zero. `send_patch`: the two entries of a CCD differ; among the 8 CCDs of one index of ccd no patch is named more than 2 times, and some patch is named exactly that often in every draw. `request_patch`: the two entries of a CCD differ; among the 8 CCDs of one index of ccd no patch is named more than 2 times, and some patch is named exactly that often in every draw.
All inputs are finite; a program needn't handle non-finite values.
Results may differ from the reference program's by a relative error of at most 0.0075.
Values may be sent and summed in bfloat16 or wider, within the bound.
No kernel may reach another device: no remote copies, remote signals or barrier semaphores. Data moves between devices by JAX's collectives and lax.ppermute only.
A program may use at most 128 MiB of HBM per device.

```python
import math
import jax
import jax.numpy as jnp
import numpy as np
from jax import lax

COLS = 4096
ROWS_DEV = 32
CCD_DEV = 8
CAP = 2
CAP2 = 2
NWARP = 2
NB = 3
TAPS = 21
TILES = 32
STRIPS = 8
CCDS = 128
PATCHES = 16
ROWS = 256
N_STRIP = 8


def banded_values(key, shape, centre_offset):
    first_key, second_key = jax.random.split(key)
    centre = jax.random.uniform(first_key, shape, jnp.float32, 0.705, 1.0)
    side = 0.076 * jax.random.truncated_normal(second_key, -2.5, 2.5, shape, jnp.float32)
    value = jnp.where(centre_offset == 0, centre, jnp.where(jnp.abs(centre_offset) <= 3, side, 0.0))
    return value.astype(jnp.bfloat16)


def draw_row_warp(key, part):
    key = jax.random.fold_in(key, 11)
    shape = (CCDS, ROWS, ROWS_DEV + 6)
    own_row = lax.broadcasted_iota(jnp.int32, shape, 1) % ROWS_DEV
    source_row = lax.broadcasted_iota(jnp.int32, shape, 2)
    return banded_values(key, shape, source_row - own_row - 3)


def draw_col_warp(key, part):
    key = jax.random.fold_in(key, 23)
    shape = (NWARP, TILES, 384, 128)
    source_col = lax.broadcasted_iota(jnp.int32, shape, 2)
    own_col = lax.broadcasted_iota(jnp.int32, shape, 3)
    return banded_values(key, shape, source_col - own_col - 128)


def place_ends(result, rng, smallest, largest):
    dims = result.shape
    place = [jax.random.randint(jax.random.fold_in(rng, axis), (), 0, dims[axis]) for axis in range(len(dims))]
    result = result.at[tuple(place)].set(smallest)
    longest = dims.index(max(dims))
    place[longest] = (place[longest] + 1) % dims[longest]
    return result.at[tuple(place)].set(largest)


def block_scale(key, extent, shards, low, largest):
    def one(dim, blocks):
        draws = jax.random.uniform(jax.random.fold_in(jax.random.fold_in(key, 6), dim), (blocks,), jnp.float32, low / len(shards), largest / len(shards))
        return jnp.repeat(jnp.exp(draws), extent[dim] // blocks).reshape((-1,) + (1,) * (len(extent) - dim - 1))

    factor_of = one(*shards[0])
    for cut in shards[1:]:
        factor_of = factor_of * one(*cut)
    return factor_of


def assign_block(key, own, number, rows, number_of, top, most, slope):
    ranking = jax.random.permutation(key, number_of)
    packed, ordinary = portions_of(number_of, rows * top, most, slope, True), portions_of(number_of, rows * top, most, slope, False)
    places = jnp.arange(number_of)

    def named(sizes, turn):
        used = int((sizes > 0).sum())
        fixed = max(1, used // 4)
        passed = fixed + (places - fixed + turn * (used - fixed)) % max(1, number_of - fixed)
        return jnp.zeros((number_of,), jnp.int32).at[ranking[jnp.where(places < fixed, places, passed)]].set(jnp.asarray(sizes, jnp.int32))

    sizes = jnp.where(number % 4 == 0, named(packed, number // 4), named(ordinary, number - number // 4 - 1))
    mixed = jax.random.permutation(jax.random.fold_in(own, 3), number_of)
    donor, sink = mixed[0:number_of // 2 * 2:2], mixed[1:number_of // 2 * 2:2]
    slack = jnp.minimum(sizes[donor] - 1, most - sizes[sink]) // 2
    slack = jnp.where((donor == ranking[0]) | (sink == ranking[0]) | (sizes[sink] == 0), 0, jnp.maximum(slack, 0))
    passed = jax.random.randint(jax.random.fold_in(own, 4), (number_of // 2,), 0, 1 << 20) % (slack + 1)
    sizes = sizes.at[donor].add(-passed).at[sink].add(passed)
    items = jnp.searchsorted(jnp.cumsum(sizes), jnp.arange(rows * top), side="right").astype(jnp.int32)
    listing = items.reshape(top, rows).T
    listing = listing[jax.random.permutation(jax.random.fold_in(own, 1), rows)]
    turn = jax.random.randint(jax.random.fold_in(own, 2), (rows, 1), 0, top)
    return jnp.take_along_axis(listing, (jnp.arange(top)[None, :] + turn) % top, axis=1)


def portions_of(number_of, total, bound, skew, full):
    portions = [(1 << 20) // math.isqrt(standing ** skew) + 1 for standing in range(1, number_of + 1)]
    largest = bound if full else min(bound, max(-(-total // number_of), total * portions[0] // sum(portions)))
    least = 1 if total - largest >= number_of - 1 else 0
    given, surplus = [largest] + [least] * (number_of - 1), total - largest - least * (number_of - 1)
    while surplus > 0:
        candidates = [i for i in range(1, number_of) if given[i] < largest] or [i for i in range(1, number_of) if given[i] < bound]
        mass, left = sum([portions[i] for i in candidates]), surplus
        for i in candidates:
            extra = min(bound - given[i], max(1, left * portions[i] // mass), surplus)
            given[i] = given[i] + extra
            surplus = surplus - extra
    return np.array(given)


def centred(rng, dims, deviation, most, shards=(), dtype=jnp.bfloat16):
    drawn = jax.random.normal(rng, dims, jnp.float32) * deviation
    if len(shards) > 0:
        drawn = block_scale(rng, dims, shards, -0.22, 0.18) * drawn
    return jnp.clip(drawn, min=-most, max=most).astype(dtype)


def setup_inputs(seed: int = 0) -> dict:
    streams_of = jax.random.split(jax.random.key(seed), 13)
    images = centred(streams_of[0], (CCDS, ROWS, COLS), 1.0, 6.0, ((0, 16), (1, 8)))
    variances = jnp.clip(jnp.exp(math.log(4.0) - 2.7725887 * jax.random.uniform(streams_of[1], (CCDS, ROWS, COLS), jnp.float32) ** block_scale(streams_of[1], (CCDS, ROWS, COLS), ((0, 16), (1, 8)), -0.2, 0.2)), 0.25, 4.0).astype(jnp.bfloat16)
    row_warp = draw_row_warp(jax.random.fold_in(streams_of[12], 71), 0)
    col_warp = draw_col_warp(jax.random.fold_in(streams_of[12], 71), 0)
    warp_index = place_ends(jax.random.randint(streams_of[4], (CCDS, STRIPS), 0, NWARP), jax.random.fold_in(streams_of[4], 1), 0, NWARP - 1).astype(jnp.int32)
    psf_kernels = centred(streams_of[5], (CCDS, NB, TAPS), 0.2, 1.1953125, ((0, 16),))
    psf_coeff = centred(streams_of[6], (CCDS, STRIPS, NB, COLS), 0.5, 3.0, ((0, 16), (1, 8)), jnp.float32)
    send_patch_keys = jax.random.split(jax.random.fold_in(streams_of[7], 1), CCDS // CCD_DEV)
    send_patch_turns = jax.random.permutation(jax.random.fold_in(streams_of[7], 3), CCDS // CCD_DEV)
    send_patch = jax.vmap(lambda own, number: assign_block(jax.random.fold_in(streams_of[7], 2), own, number, CCD_DEV, PATCHES, 2, CAP, 2))(send_patch_keys, send_patch_turns).reshape((CCDS, 2))
    send_offset = place_ends(jax.random.randint(streams_of[8], (CCDS, 2), 0, ROWS_DEV), jax.random.fold_in(streams_of[8], 1), 0, ROWS_DEV - 1).astype(jnp.int32)
    request_patch_keys = jax.random.split(jax.random.fold_in(streams_of[9], 1), CCDS // CCD_DEV)
    request_patch_turns = jax.random.permutation(jax.random.fold_in(streams_of[9], 3), CCDS // CCD_DEV)
    request_patch = jax.vmap(lambda own, number: assign_block(jax.random.fold_in(streams_of[9], 2), own, number, CCD_DEV, PATCHES, 2, CAP2, 2))(request_patch_keys, request_patch_turns).reshape((CCDS, 2))
    request_offset = place_ends(jax.random.randint(streams_of[10], (CCDS, 2), 0, ROWS_DEV), jax.random.fold_in(streams_of[10], 1), 0, ROWS_DEV - 1).astype(jnp.int32)
    new_images = centred(streams_of[11], (CCDS, ROWS, COLS), 1.0, 6.0, ((0, 16), (1, 8)))
    return dict(images=images, variances=variances, row_warp=row_warp, col_warp=col_warp, warp_index=warp_index, psf_kernels=psf_kernels, psf_coeff=psf_coeff, send_patch=send_patch, send_offset=send_offset, request_patch=request_patch, request_offset=request_offset, new_images=new_images)


def warp_columns(row_block, warp_table):
    row_count, col_count = row_block.shape
    tile_rows = row_block.astype(jnp.float32).reshape(row_count, col_count // 128, 128)
    zero_tile = jnp.zeros((row_count, 1, 128), jnp.float32)
    before = jnp.concatenate([zero_tile, tile_rows[:, :-1]], axis=1)
    following = jnp.concatenate([tile_rows[:, 1:], zero_tile], axis=1)
    table_wide = warp_table.astype(jnp.float32)
    summed = jnp.einsum("rtk,tkl->rtl", before, table_wide[:, 0:128], precision=lax.Precision.HIGHEST)
    summed = summed + jnp.einsum("rtk,tkl->rtl", tile_rows, table_wide[:, 128:256], precision=lax.Precision.HIGHEST)
    summed = summed + jnp.einsum("rtk,tkl->rtl", following, table_wide[:, 256:384], precision=lax.Precision.HIGHEST)
    return summed.reshape(row_count, col_count)


def psf_match(warped, kernels, coefficients):
    col_count = warped.shape[1]
    tap_count = kernels.shape[1]
    half_width = tap_count // 2
    values = warped.astype(jnp.float32)
    padded = jnp.pad(values, ((0, 0), (half_width, half_width)))
    matched = values
    for basis_index in range(kernels.shape[0]):
        convolved = jnp.zeros_like(values)
        for tap_index in range(tap_count):
            convolved = convolved + kernels[basis_index, tap_index].astype(jnp.float32) * padded[:, tap_index:tap_index + col_count]
        matched = matched + coefficients[basis_index] * convolved
    return matched


def one_ccd(ccd_image, ccd_variance, warp_rows, indices, kernels, coefficients, col_warp):
    padded = jnp.pad(jnp.stack([ccd_image, ccd_variance]), ((0, 0), (3, 3), (0, 0)))
    flux_parts = []
    weight_parts = []
    for strip_index in range(N_STRIP):
        first_row = strip_index * ROWS_DEV
        window = padded[:, first_row:first_row + ROWS_DEV + 6]
        row_matrix = warp_rows[first_row:first_row + ROWS_DEV]
        row_squares = (row_matrix.astype(jnp.float32) * row_matrix.astype(jnp.float32)).astype(jnp.bfloat16)
        image_rows = jnp.dot(row_matrix, window[0], preferred_element_type=jnp.float32).astype(jnp.bfloat16)
        variance_rows = jnp.dot(row_squares, window[1], preferred_element_type=jnp.float32).astype(jnp.bfloat16)
        warp_table = lax.dynamic_index_in_dim(col_warp, indices[strip_index], 0, keepdims=False)
        table_squares = (warp_table.astype(jnp.float32) * warp_table.astype(jnp.float32)).astype(jnp.bfloat16)
        warped = warp_columns(image_rows, warp_table).astype(jnp.bfloat16)
        variance_warped = warp_columns(variance_rows, table_squares)
        matched = psf_match(warped, kernels, coefficients[strip_index])
        inverse = 1.0 / variance_warped
        flux_parts.append((matched * inverse).astype(jnp.bfloat16))
        weight_parts.append(inverse.astype(jnp.bfloat16))
    return jnp.concatenate(flux_parts, axis=0), jnp.concatenate(weight_parts, axis=0)


def reference(images, variances, row_warp, col_warp, warp_index, psf_kernels, psf_coeff, send_patch, send_offset, request_patch, request_offset, new_images):
    def accumulate(running, ccd_inputs):
        numerator, denominator = running
        ccd_image, ccd_variance, warp_rows, indices, kernels, coefficients, patches, offsets = ccd_inputs
        flux_rows, weight_rows = one_ccd(ccd_image, ccd_variance, warp_rows, indices, kernels, coefficients, col_warp)
        flux_wide = flux_rows.astype(jnp.float32)
        weight_wide = weight_rows.astype(jnp.float32)
        for route_index in range(2):
            numerator = numerator.at[patches[route_index]].add(jnp.roll(flux_wide, offsets[route_index], axis=0))
            denominator = denominator.at[patches[route_index]].add(jnp.roll(weight_wide, offsets[route_index], axis=0))
        return (numerator, denominator), None

    empty_sum = jnp.zeros((PATCHES, ROWS, COLS), jnp.float32)
    (numerator, denominator), _ = lax.scan(accumulate, (empty_sum, empty_sum), (images, variances, row_warp, warp_index, psf_kernels, psf_coeff, send_patch, send_offset))
    patch_coadd = (numerator / (1.0 + denominator)).astype(jnp.bfloat16)
    half_cols = COLS // 2

    def one_template(inputs):
        patches, offsets = inputs
        pieces = []
        for side_index in range(2):
            source = lax.dynamic_index_in_dim(patch_coadd, patches[side_index], 0, keepdims=False)
            rolled = jnp.roll(source, -offsets[side_index], axis=0)
            pieces.append(rolled[:, side_index * half_cols:(side_index + 1) * half_cols])
        return jnp.concatenate(pieces, axis=1)

    template = lax.map(one_template, (request_patch, request_offset))
    difference = (new_images.astype(jnp.float32) - template.astype(jnp.float32)).astype(jnp.bfloat16)
    return patch_coadd, difference
```

```python
import functools

import jax
import jax.numpy as jnp
from jax import lax
from jax.experimental import pallas as pl
from jax.experimental.pallas import tpu as pltpu
from jax.sharding import PartitionSpec as P

TILE = 128
SIDE = 4
HALF = 16
CHUNKS = 2
F32 = jnp.float32
BF16 = jnp.bfloat16
VMEM_LIMIT = 40 * 1024 * 1024


def strip_shift(value, steps, wrap=True):
    count = lax.axis_size("strip")
    pairs = [(i, (i + steps) % count) for i in range(count) if wrap or 0 <= i + steps < count]
    return lax.ppermute(value, "strip", pairs)


def plane_shift(value, axis, steps):
    pairs = []
    for i in range(SIDE * SIDE):
        y, x = divmod(i, SIDE)
        if axis == "x":
            x = (x + steps) % SIDE
        else:
            y = (y + steps) % SIDE
        pairs.append((i, y * SIDE + x))
    return lax.ppermute(value, "ccd", pairs)


def dot(a, b):
    return jnp.dot(a, b, preferred_element_type=F32)


def squared(values):
    wide = values.astype(F32)
    return (wide * wide).astype(BF16)


def ccd_kernel(
    first,
    width,
    columns,
    pick_ref,
    main_ref,
    edge_ref,
    bands_ref,
    images_hbm,
    variances_hbm,
    before_hbm,
    after_hbm,
    table_hbm,
    coeff_hbm,
    low_ref,
    high_ref,
    pixels,
    rims,
    table,
    coeff,
    rowed,
    warped,
    inverse,
    sems,
):
    tiles = width // TILE
    all_tiles = columns // TILE
    t0 = first // TILE
    start = max(first - 2 * TILE, 0)
    stop = min(first + width + 2 * TILE, columns)
    span = stop - start
    table_start = max(t0 - 1, 0)
    table_stop = min(t0 + tiles + 1, all_tiles)
    rows = main_ref.shape[1]
    ccds = rows // 32
    cols = pl.ds(start, span)
    edge_rows = before_hbm.shape[0]
    copies = [
        pltpu.make_async_copy(images_hbm.at[:, cols], pixels.at[0], sems.at[0]),
        pltpu.make_async_copy(variances_hbm.at[:, cols], pixels.at[1], sems.at[1]),
        pltpu.make_async_copy(before_hbm.at[:, cols], rims.at[pl.ds(0, edge_rows)], sems.at[2]),
        pltpu.make_async_copy(
            after_hbm.at[:, cols], rims.at[pl.ds(edge_rows, edge_rows)], sems.at[3]
        ),
        pltpu.make_async_copy(
            table_hbm.at[:, pl.ds(table_start, table_stop - table_start), pl.ds(64, 256), :],
            table,
            sems.at[4],
        ),
        pltpu.make_async_copy(coeff_hbm.at[:, :, pl.ds(first, width)], coeff, sems.at[5]),
    ]
    for copy in copies:
        copy.start()
    shift = (start - (first - 2 * TILE)) // TILE
    if shift > 0:
        rowed[:, 0:shift] = jnp.zeros((2, shift, rows, TILE), BF16)
    end = shift + span // TILE
    if end < tiles + 4:
        rowed[:, end : tiles + 4] = jnp.zeros((2, tiles + 4 - end, rows, TILE), BF16)
    for copy in copies[:4]:
        copy.wait()

    def row_step(j, carry):
        here = pl.ds(pl.multiple_of(j * 256, 256), 256)
        edges = rims[:, here]
        for kind in range(2):
            out = dot(main_ref[kind], pixels[kind, :, here]) + dot(edge_ref[kind], edges)
            out = out.astype(BF16)
            rowed[kind, shift + 2 * j] = out[:, :TILE]
            rowed[kind, shift + 2 * j + 1] = out[:, TILE:]
        return carry

    lax.fori_loop(0, span // 256, row_step, 0)
    copies[4].wait()
    lane = lax.broadcasted_iota(jnp.int32, (rows, TILE), 1)

    def with_halo(own, previous, following):
        halo = jnp.where(lane[: own.shape[0]] < 64, following, previous)
        return jnp.concatenate([own, halo], axis=1)

    def weights(k):
        parts = []
        for m in range(2):
            part = table[m, k]
            parts.append(jnp.concatenate([part[64:192], part[192:256], part[0:64]], axis=0))
        return jnp.concatenate(parts, axis=1)

    def choose(product, c):
        block = product[c * 32 : (c + 1) * 32]
        return jnp.where(pick_ref[c] == 0, block[:, :TILE], block[:, TILE:])

    def column_step(w, with_variance):
        matrix = weights(w + (t0 - 1 - table_start))
        product = dot(with_halo(rowed[0, w + 1], rowed[0, w], rowed[0, w + 2]), matrix)
        at = pl.ds(pl.multiple_of(w * 32, 32), 32)
        for c in range(ccds):
            warped[c, at] = choose(product, c).astype(BF16)
        if with_variance:
            product = dot(
                with_halo(rowed[1, w + 1], rowed[1, w], rowed[1, w + 2]), squared(matrix)
            )
            at = pl.ds(pl.multiple_of((w - 1) * 32, 32), 32)
            for c in range(ccds):
                inverse[c, at] = 1.0 / choose(product, c)

    for w in (0, tiles + 1):
        if 0 <= t0 - 1 + w < all_tiles:
            column_step(w, False)
        else:
            warped[:, w * 32 : (w + 1) * 32] = jnp.zeros((ccds, 32, TILE), BF16)

    def column_loop(w, carry):
        column_step(w, True)
        return carry

    lax.fori_loop(1, tiles + 1, column_loop, 0)
    copies[5].wait()
    group = 8

    def ccd_step(c, carry):
        row16 = pl.ds(pl.multiple_of(c * HALF, HALF), HALF)
        for g in range(tiles // group):
            base = g * group * 32
            size = group * 32
            own = warped[c, base + 32 : base + 32 + size]
            lhs = with_halo(
                own, warped[c, base : base + size], warped[c, base + 64 : base + 64 + size]
            )
            convolved = dot(lhs, bands_ref[c])
            for k in range(group):
                tile = g * group + k
                here = slice(k * 32, (k + 1) * 32)
                matched = own[here].astype(F32)
                for b in range(3):
                    factor = coeff[c, b : b + 1, tile * TILE : (tile + 1) * TILE]
                    matched = matched + factor * convolved[here, b * TILE : (b + 1) * TILE]
                weight = inverse[c, tile * 32 : (tile + 1) * 32]
                flux = (matched * weight).astype(BF16)
                weight = weight.astype(BF16)
                left = slice(tile * TILE, (tile + 1) * TILE)
                right = slice(width + tile * TILE, width + (tile + 1) * TILE)
                low_ref[row16, left] = flux[:HALF]
                high_ref[row16, left] = flux[HALF:]
                low_ref[row16, right] = weight[:HALF]
                high_ref[row16, right] = weight[HALF:]
        return carry

    lax.fori_loop(0, ccds, ccd_step, 0)


def ccd_block(
    first, width, pick, main, edge, bands, images, variances, before, after, col_warp, coeff
):
    rows, columns = images.shape
    tiles = width // TILE
    span = min(first + width + 2 * TILE, columns) - max(first - 2 * TILE, 0)
    table_tiles = min(first // TILE + tiles + 1, columns // TILE) - max(first // TILE - 1, 0)
    ccds = rows // 32
    vmem = pl.BlockSpec(memory_space=pltpu.VMEM)
    anywhere = pl.BlockSpec(memory_space=pl.ANY)
    out = jax.ShapeDtypeStruct((rows // 2, 2 * width), BF16)
    return pl.pallas_call(
        functools.partial(ccd_kernel, first, width, columns),
        out_shape=(out, out),
        in_specs=[pl.BlockSpec(memory_space=pltpu.SMEM)] + [vmem] * 3 + [anywhere] * 6,
        out_specs=(vmem, vmem),
        scratch_shapes=[
            pltpu.VMEM((2, rows, span), BF16),
            pltpu.VMEM((2 * before.shape[0], span), BF16),
            pltpu.VMEM((2, table_tiles, 256, TILE), BF16),
            pltpu.VMEM((ccds, 3, width), F32),
            pltpu.VMEM((2, tiles + 4, rows, TILE), BF16),
            pltpu.VMEM((ccds, (tiles + 2) * 32, TILE), BF16),
            pltpu.VMEM((ccds, tiles * 32, TILE), F32),
            pltpu.SemaphoreType.DMA((6,)),
        ],
        compiler_params=pltpu.CompilerParams(vmem_limit_bytes=VMEM_LIMIT),
        cost_estimate=pl.CostEstimate(
            flops=2 * rows * width * 256 * 9, bytes_accessed=rows * width * 16, transcendentals=0
        ),
    )(pick, main, edge, bands, images, variances, before, after, col_warp, coeff)


def far_kernel(blocks, select_ref, a_ref, b_ref, c_ref, d_ref, flux_ref, weight_ref):
    j = pl.program_id(0)
    stack = jnp.concatenate([a_ref[...], b_ref[...], c_ref[...], d_ref[...]], axis=0)
    out = dot(select_ref[...], stack).astype(BF16)

    @pl.when(j < blocks)
    def _():
        flux_ref[...] = out

    @pl.when(j >= blocks)
    def _():
        weight_ref[...] = out


def far_sums(select, sources):
    height, width = sources[0].shape
    rows, depth = select.shape
    step = min(1024, width // 2)
    blocks = width // 2 // step
    out = jax.ShapeDtypeStruct((rows, width // 2), BF16)
    return pl.pallas_call(
        functools.partial(far_kernel, blocks),
        grid=(2 * blocks,),
        out_shape=(out, out),
        in_specs=[pl.BlockSpec((rows, depth), lambda j: (0, 0))]
        + [pl.BlockSpec((height, step), lambda j: (0, j))] * 4,
        out_specs=(
            pl.BlockSpec((rows, step), lambda j: (0, jnp.minimum(j, blocks - 1))),
            pl.BlockSpec((rows, step), lambda j: (0, jnp.maximum(j - blocks, 0))),
        ),
        compiler_params=pltpu.CompilerParams(vmem_limit_bytes=VMEM_LIMIT),
        cost_estimate=pl.CostEstimate(
            flops=2 * rows * depth * width, bytes_accessed=width * 1280, transcendentals=0
        ),
    )(select, *sources)


def near_kernel(select_ref, a_ref, b_ref, c_ref, d_ref, *out_refs):
    stack = jnp.concatenate([a_ref[...], b_ref[...], c_ref[...], d_ref[...]], axis=0)
    out = dot(select_ref[...], stack).astype(BF16)
    rows = out_refs[0].shape[0]
    for k, out_ref in enumerate(out_refs):
        out_ref[...] = out[k * rows : (k + 1) * rows]


def near_sums(select, sources):
    height, width = sources[0].shape
    rows, depth = select.shape
    step = min(1024, width)
    out = jax.ShapeDtypeStruct((rows // 3, width), BF16)
    return pl.pallas_call(
        near_kernel,
        grid=(width // step,),
        out_shape=(out,) * 3,
        in_specs=[pl.BlockSpec((rows, depth), lambda j: (0, 0))]
        + [pl.BlockSpec((height, step), lambda j: (0, j))] * 4,
        out_specs=(pl.BlockSpec((rows // 3, step), lambda j: (0, j)),) * 3,
        compiler_params=pltpu.CompilerParams(vmem_limit_bytes=VMEM_LIMIT),
        cost_estimate=pl.CostEstimate(
            flops=2 * rows * depth * width, bytes_accessed=width * 1792, transcendentals=0
        ),
    )(select, *sources)


def patch_stack(j, blocks, own_ref, next_ref, last_ref, left_ref, right_ref):
    far = jnp.where(j < blocks // 2, left_ref[...], right_ref[...])
    return jnp.concatenate([own_ref[...], next_ref[...], last_ref[...], far], axis=0)


def lend_kernel(blocks, select_ref, *refs):
    out = dot(select_ref[...], patch_stack(pl.program_id(0), blocks, *refs[:5])).astype(BF16)
    rows = out.shape[0] // 2
    refs[5][...] = out[:rows]
    refs[6][...] = out[rows:]


def patch_specs(height, step, blocks):
    half = blocks // 2
    return [pl.BlockSpec((height, step), lambda j: (0, j))] * 3 + [
        pl.BlockSpec((height, step), lambda j: (0, jnp.minimum(j, half - 1))),
        pl.BlockSpec((height, step), lambda j: (0, jnp.maximum(j - half, 0))),
    ]


def lent_rows(select, patches):
    height, width = patches[0].shape
    rows, depth = select.shape
    step = min(1024, width // 2)
    blocks = width // step
    out = jax.ShapeDtypeStruct((rows // 2, width), BF16)
    return pl.pallas_call(
        functools.partial(lend_kernel, blocks),
        grid=(blocks,),
        out_shape=(out, out),
        in_specs=[pl.BlockSpec((rows, depth), lambda j: (0, 0))]
        + patch_specs(height, step, blocks),
        out_specs=(pl.BlockSpec((rows // 2, step), lambda j: (0, j)),) * 2,
        compiler_params=pltpu.CompilerParams(vmem_limit_bytes=VMEM_LIMIT),
        cost_estimate=pl.CostEstimate(
            flops=2 * rows * depth * width, bytes_accessed=width * 1536, transcendentals=0
        ),
    )(select, *patches)


def difference_kernel(blocks, select_ref, *refs):
    new_ref, down_ref, up_ref, out_ref = refs[5], refs[6], refs[7], refs[-1]
    own = dot(select_ref[...], patch_stack(pl.program_id(0), blocks, *refs[:5]))
    count = new_ref.shape[0]
    for c in range(count):
        here = slice(c * HALF, (c + 1) * HALF)
        there = slice((count + c) * HALF, (count + c + 1) * HALF)
        low = own[here] + down_ref[here].astype(F32)
        high = own[there] + up_ref[here].astype(F32)
        out_ref[c, 0:HALF] = (new_ref[c, 0:HALF].astype(F32) - low).astype(BF16)
        out_ref[c, HALF : 2 * HALF] = (new_ref[c, HALF : 2 * HALF].astype(F32) - high).astype(BF16)


def difference_block(first, select, patches, new_images, down, up, running):
    height, width = patches[0].shape
    rows, depth = select.shape
    step = min(1024, width // 2)
    blocks = width // step
    count, strip_rows, columns = new_images.shape
    offset = first // step
    place = pl.BlockSpec((count, strip_rows, step), lambda j: (0, 0, j + offset))
    lent = pl.BlockSpec((down.shape[0], step), lambda j: (0, j))
    operands = [select, *patches, new_images, down, up]
    specs = [pl.BlockSpec((rows, depth), lambda j: (0, 0))]
    specs += patch_specs(height, step, blocks) + [place, lent, lent]
    aliases = {}
    if running is not None:
        aliases = {len(operands): 0}
        operands.append(running)
        specs.append(pl.BlockSpec(memory_space=pl.ANY))
    return pl.pallas_call(
        functools.partial(difference_kernel, blocks),
        grid=(blocks,),
        out_shape=jax.ShapeDtypeStruct(new_images.shape, BF16),
        in_specs=specs,
        out_specs=place,
        input_output_aliases=aliases,
        compiler_params=pltpu.CompilerParams(vmem_limit_bytes=VMEM_LIMIT),
        cost_estimate=pl.CostEstimate(
            flops=2 * rows * depth * width, bytes_accessed=width * 2560, transcendentals=0
        ),
    )(*operands)


def row_matrices(row_warp):
    count, rows, _ = row_warp.shape
    same = jnp.eye(count, dtype=bool)[:, None, :, None]

    def spread(part):
        return jnp.where(same, part[:, :, None, :], jnp.zeros((), BF16))

    mains, edges = [], []
    for kind, matrix in enumerate((row_warp, squared(row_warp))):
        mains.append(spread(matrix[:, :, 3:35]).reshape(count * rows, count * 32))
        empty = jnp.zeros((count * rows, count * 3), BF16)
        sides = []
        for part in (matrix[:, :, 0:3], matrix[:, :, 35:38]):
            block = spread(part).reshape(count * rows, count * 3)
            sides += [block, empty] if kind == 0 else [empty, block]
        edges.append(jnp.concatenate(sides, axis=1))
    return jnp.stack(mains), jnp.stack(edges)


def kernel_bands(kernels):
    count, basis, taps = kernels.shape
    inside = lax.broadcasted_iota(jnp.int32, (taps, 256, TILE), 1)
    source = jnp.where(inside < 192, inside, inside - 256)
    target = lax.broadcasted_iota(jnp.int32, (taps, 256, TILE), 2)
    tap = lax.broadcasted_iota(jnp.int32, (taps, 256, TILE), 0)
    picks = (source - target + taps // 2 == tap).astype(BF16)
    bands = jnp.einsum("cbu,ukl->ckbl", kernels, picks, preferred_element_type=F32)
    return bands.astype(BF16).reshape(count, 256, basis * TILE)


def selection(patches, offsets, order, position):
    base_y, base_x = position // SIDE, position % SIDE
    names = jnp.stack(
        [(base_y + dy) % SIDE * SIDE + (base_x + dx) % SIDE for dx, dy in order]
    ).astype(jnp.int32)
    row = jnp.arange(2 * HALF, dtype=jnp.int32)
    within = jnp.arange(HALF, dtype=jnp.int32)
    place = jnp.stack([within, within + HALF, within + 2 * HALF, within - HALF])
    hit = patches[None, :] == names[:, None]
    meets = (HALF + row[:, None, None, None] - offsets[None, None, :, None]) == place[
        None, :, None, :
    ]
    return hit[:, None, None, :, None] & meets[None]


def body(
    images,
    variances,
    row_warp,
    col_warp,
    warp_index,
    psf_kernels,
    psf_coeff,
    send_patch,
    send_offset,
    request_patch,
    request_offset,
    new_images,
):
    count, rows, columns = images.shape
    flat = count * rows
    width = columns // CHUNKS
    position = lax.axis_index("ccd")

    def ends(cut):
        return jnp.concatenate(
            [cut(images).reshape(count * 3, columns), cut(variances).reshape(count * 3, columns)],
            axis=0,
        )

    before = strip_shift(ends(lambda a: a[:, rows - 3 :]), 1, wrap=False)
    after = strip_shift(ends(lambda a: a[:, :3]), -1, wrap=False)
    main, edge = row_matrices(row_warp)
    bands = kernel_bands(psf_kernels)
    plain = images.reshape(flat, columns), variances.reshape(flat, columns)

    orders = [
        [(dx, dy) for dx in (2, 1, 3, 0) for dy in range(SIDE)],
        [(dx, dy) for dy in (2, 1, 3, 0) for dx in range(SIDE)],
    ]
    axes = [("x", "y"), ("y", "x")]
    sends, asks = [], []
    for order in orders:
        hit = selection(send_patch[:, 0], send_offset[:, 0], order, position)
        hit = hit | selection(send_patch[:, 1], send_offset[:, 1], order, position)
        sends.append(hit.astype(BF16).reshape(16 * 32, 4 * count * HALF))
    for j in range(CHUNKS):
        h = j * 2 // CHUNKS
        order = orders[j % 2]
        order = order[12:] + order[4:12] + order[:4]
        ask = selection(request_patch[:, h], request_offset[:, h], order, position)
        asks.append(
            ask.astype(BF16).transpose(2, 3, 4, 0, 1).reshape(4 * count * HALF, 16 * 32)
        )

    sources = []
    for j in range(CHUNKS):
        low, high = ccd_block(
            j * width,
            width,
            warp_index[:, 0],
            main,
            edge,
            bands,
            *plain,
            before,
            after,
            col_warp,
            psf_coeff[:, 0],
        )
        sources.append((low, high, strip_shift(low, -1), strip_shift(high, 1)))

    def added(*terms):
        total = terms[0].astype(F32)
        for term in terms[1:]:
            total = total + term.astype(F32)
        return total

    coadds, gathered = [], []
    for j in range(CHUNKS):
        first_axis, second_axis = axes[j % 2]
        select = sends[j % 2]
        far_flux, far_weight = far_sums(select[:128], sources[j])
        from_low = plane_shift(far_flux, first_axis, 1)
        from_high = plane_shift(far_weight, first_axis, -1)
        ahead, behind, own = near_sums(select[128:], sources[j])
        ahead = jnp.concatenate(
            [added(ahead[:, :width], from_low).astype(BF16), ahead[:, width:]], axis=1
        )
        behind = jnp.concatenate(
            [behind[:, :width], added(behind[:, width:], from_high).astype(BF16)], axis=1
        )
        from_low = plane_shift(ahead, first_axis, 1)
        from_high = plane_shift(behind, first_axis, -1)
        own = added(own, from_low, from_high).astype(BF16)
        from_low = plane_shift(own[64:96, :width], second_axis, 1)
        from_high = plane_shift(own[64:96, width:], second_axis, -1)
        ahead = jnp.concatenate(
            [added(own[32:64, :width], from_low).astype(BF16), own[32:64, width:]], axis=1
        )
        behind = jnp.concatenate(
            [own[96:, :width], added(own[96:, width:], from_high).astype(BF16)], axis=1
        )
        from_low = plane_shift(ahead, second_axis, 1)
        from_high = plane_shift(behind, second_axis, -1)
        total = added(own[:32], from_low, from_high)
        coadd = (total[:, :width] / (1.0 + total[:, width:])).astype(BF16)
        coadds.append(coadd)

    for j in range(CHUNKS):
        first_axis, second_axis = axes[j % 2]
        half = width // 2

        def spread(block, axis):
            last = plane_shift(block, axis, 1)
            following = plane_shift(block, axis, -1)
            left = plane_shift(last[:, :half], axis, 1)
            right = plane_shift(following[:, half:], axis, -1)
            return following, last, left, right

        following, last, left, right = spread(coadds[j], second_axis)
        block = jnp.concatenate(
            [coadds[j], following, jnp.concatenate([left, right], axis=1), last], axis=0
        )
        gathered.append((block, *spread(block, first_axis)))

    difference = None
    for j in range(CHUNKS):
        ask = asks[j]
        down, up = lent_rows(ask[256:], gathered[j])
        down = strip_shift(down, 1)
        up = strip_shift(up, -1)
        difference = difference_block(
            j * width, ask[:256], gathered[j], new_images, down, up, difference
        )

    window = jnp.concatenate(coadds, axis=1)
    patch_coadd = jnp.concatenate([strip_shift(window[HALF:], 1), window[:HALF]], axis=0)
    return (patch_coadd[None], difference)


def solution(mesh):
    return jax.shard_map(
        body,
        mesh=mesh,
        in_specs=(
            P("ccd", "strip", None),
            P("ccd", "strip", None),
            P("ccd", "strip", None),
            P(),
            P("ccd", "strip"),
            P("ccd", None, None),
            P("ccd", "strip", None, None),
            P("ccd", None),
            P("ccd", None),
            P("ccd", None),
            P("ccd", None),
            P("ccd", "strip", None),
        ),
        out_specs=(P("ccd", "strip", None), P("ccd", "strip", None)),
        check_vma=False,
    )
```

```python
import functools

import jax
import jax.numpy as jnp
from jax import lax
from jax.experimental import pallas as pl
from jax.experimental.pallas import tpu as pltpu
from jax.sharding import PartitionSpec as P

TILE = 128
SIDE = 4
HALF = 16
BOUNDS = (0, 2304, 4096)
F32 = jnp.float32
BF16 = jnp.bfloat16
VMEM_LIMIT = 40 * 1024 * 1024


def strip_shift(value, steps, wrap=True):
    count = lax.axis_size("strip")
    pairs = [(i, (i + steps) % count) for i in range(count) if wrap or 0 <= i + steps < count]
    return lax.ppermute(value, "strip", pairs)


def plane_shift(value, axis, steps):
    pairs = []
    for i in range(SIDE * SIDE):
        y, x = divmod(i, SIDE)
        if axis == "x":
            x = (x + steps) % SIDE
        else:
            y = (y + steps) % SIDE
        pairs.append((i, y * SIDE + x))
    return lax.ppermute(value, "ccd", pairs)


def dot(a, b):
    return jnp.dot(a, b, preferred_element_type=F32)


def in_hbm(value):
    return pltpu.with_memory_space_constraint(value, pltpu.HBM)


def squared(values):
    wide = values.astype(F32)
    return (wide * wide).astype(BF16)


HINT = pl.CostEstimate(flops=1, bytes_accessed=1, transcendentals=0)


def vmem_call(kernel, shapes, operands, ahead=()):
    count = len(operands)

    def ordered(*refs):
        kernel(*refs[:count], *refs[count + len(ahead) :])

    vmem = pl.BlockSpec(memory_space=pltpu.VMEM)
    return pl.pallas_call(
        ordered,
        out_shape=[jax.ShapeDtypeStruct(shape, dtype) for shape, dtype in shapes],
        in_specs=[vmem] * count + [pl.BlockSpec(memory_space=pl.ANY)] * len(ahead),
        out_specs=[vmem] * len(shapes),
        compiler_params=pltpu.CompilerParams(vmem_limit_bytes=VMEM_LIMIT),
        cost_estimate=HINT,
    )(*operands, *ahead)


def ccd_kernel(
    first,
    width,
    columns,
    pick_ref,
    main_ref,
    edge_ref,
    bands_ref,
    images_hbm,
    variances_hbm,
    before_hbm,
    after_hbm,
    table_hbm,
    coeff_hbm,
    low_ref,
    high_ref,
    pixels,
    rims,
    table,
    coeff,
    rowed,
    warped,
    inverse,
    sems,
):
    tiles = width // TILE
    all_tiles = columns // TILE
    t0 = first // TILE
    start = max(first - 2 * TILE, 0)
    stop = min(first + width + 2 * TILE, columns)
    span = stop - start
    table_start = max(t0 - 1, 0)
    table_stop = min(t0 + tiles + 1, all_tiles)
    rows = main_ref.shape[1]
    ccds = rows // 32
    edge_rows = before_hbm.shape[0]
    pieces = [(0, 768), (768, span - 768)]
    loads = []
    for p, (at, size) in enumerate(pieces):
        here, there = pl.ds(at, size), pl.ds(start + at, size)
        loads.append(
            [
                pltpu.make_async_copy(
                    images_hbm.at[:, there], pixels.at[0, :, here], sems.at[4 * p]
                ),
                pltpu.make_async_copy(
                    variances_hbm.at[:, there], pixels.at[1, :, here], sems.at[4 * p + 1]
                ),
                pltpu.make_async_copy(
                    before_hbm.at[:, there], rims.at[pl.ds(0, edge_rows), here], sems.at[4 * p + 2]
                ),
                pltpu.make_async_copy(
                    after_hbm.at[:, there],
                    rims.at[pl.ds(edge_rows, edge_rows), here],
                    sems.at[4 * p + 3],
                ),
            ]
        )
    load_table = pltpu.make_async_copy(
        table_hbm.at[:, pl.ds(table_start, table_stop - table_start), pl.ds(64, 256), :],
        table,
        sems.at[8],
    )
    load_coeff = pltpu.make_async_copy(
        coeff_hbm.at[:, 0, :, pl.ds(first, width)], coeff, sems.at[9]
    )
    for copy in loads[0] + loads[1] + [load_table, load_coeff]:
        copy.start()
    shift = (start - (first - 2 * TILE)) // TILE
    if shift > 0:
        rowed[:, 0:shift] = jnp.zeros((2, shift, rows, TILE), BF16)
    end = shift + span // TILE
    if end < tiles + 4:
        rowed[:, end : tiles + 4] = jnp.zeros((2, tiles + 4 - end, rows, TILE), BF16)
    for (at, size), copies in zip(pieces, loads):
        for copy in copies:
            copy.wait()
        for j in range(at // 256, (at + size) // 256):
            here = slice(j * 256, (j + 1) * 256)
            edges = rims[:, here]
            for kind in range(2):
                out = dot(main_ref[kind], pixels[kind, :, here]) + dot(edge_ref[kind], edges)
                out = out.astype(BF16)
                rowed[kind, shift + 2 * j] = out[:, :TILE]
                rowed[kind, shift + 2 * j + 1] = out[:, TILE:]
    load_table.wait()
    lane = lax.broadcasted_iota(jnp.int32, (rows, TILE), 1)

    def with_halo(own, previous, following):
        halo = jnp.where(lane[: own.shape[0]] < 64, following, previous)
        return jnp.concatenate([own, halo], axis=1)

    def weights(k):
        parts = []
        for m in range(2):
            part = table[m, k]
            parts.append(jnp.concatenate([part[64:192], part[192:256], part[0:64]], axis=0))
        return jnp.concatenate(parts, axis=1)

    def choose(product, c):
        block = product[c * 32 : (c + 1) * 32]
        return jnp.where(pick_ref[c] == 0, block[:, :TILE], block[:, TILE:])

    def column_step(w, with_variance):
        matrix = weights(w + (t0 - 1 - table_start))
        product = dot(with_halo(rowed[0, w + 1], rowed[0, w], rowed[0, w + 2]), matrix)
        at = pl.ds(pl.multiple_of(w * 32, 32), 32)
        for c in range(ccds):
            warped[c, at] = choose(product, c).astype(BF16)
        if with_variance:
            product = dot(
                with_halo(rowed[1, w + 1], rowed[1, w], rowed[1, w + 2]), squared(matrix)
            )
            at = pl.ds(pl.multiple_of((w - 1) * 32, 32), 32)
            for c in range(ccds):
                inverse[c, at] = 1.0 / choose(product, c)

    for w in (0, tiles + 1):
        if 0 <= t0 - 1 + w < all_tiles:
            column_step(w, False)
        else:
            warped[:, w * 32 : (w + 1) * 32] = jnp.zeros((ccds, 32, TILE), BF16)

    def column_loop(w, carry):
        column_step(w, True)
        return carry

    lax.fori_loop(1, tiles + 1, column_loop, 0, unroll=tiles // 2)
    load_coeff.wait()
    group = tiles // -(-tiles // 8)

    def ccd_step(c, carry):
        row16 = pl.ds(pl.multiple_of(c * HALF, HALF), HALF)
        for g in range(tiles // group):
            base = g * group * 32
            size = group * 32
            own = warped[c, base + 32 : base + 32 + size]
            lhs = with_halo(
                own, warped[c, base : base + size], warped[c, base + 64 : base + 64 + size]
            )
            convolved = dot(lhs, bands_ref[c])
            for k in range(group):
                tile = g * group + k
                here = slice(k * 32, (k + 1) * 32)
                matched = own[here].astype(F32)
                for b in range(3):
                    factor = coeff[c, b : b + 1, tile * TILE : (tile + 1) * TILE]
                    matched = matched + factor * convolved[here, b * TILE : (b + 1) * TILE]
                weight = inverse[c, tile * 32 : (tile + 1) * 32]
                flux = (matched * weight).astype(BF16)
                weight = weight.astype(BF16)
                left = slice(tile * TILE, (tile + 1) * TILE)
                right = slice(width + tile * TILE, width + (tile + 1) * TILE)
                low_ref[row16, left] = flux[:HALF]
                high_ref[row16, left] = flux[HALF:]
                low_ref[row16, right] = weight[:HALF]
                high_ref[row16, right] = weight[HALF:]
        return carry

    lax.fori_loop(0, ccds, ccd_step, 0, unroll=ccds)


def ccd_block(
    first, width, pick, main, edge, bands, images, variances, before, after, col_warp, coeff
):
    rows, columns = images.shape
    tiles = width // TILE
    span = min(first + width + 2 * TILE, columns) - max(first - 2 * TILE, 0)
    table_tiles = min(first // TILE + tiles + 1, columns // TILE) - max(first // TILE - 1, 0)
    ccds = rows // 32
    vmem = pl.BlockSpec(memory_space=pltpu.VMEM)
    anywhere = pl.BlockSpec(memory_space=pl.ANY)
    hbm = pl.BlockSpec(memory_space=pltpu.HBM)
    out = jax.ShapeDtypeStruct((rows // 2, 2 * width), BF16)
    return pl.pallas_call(
        functools.partial(ccd_kernel, first, width, columns),
        out_shape=(out, out),
        in_specs=[pl.BlockSpec(memory_space=pltpu.SMEM)] + [vmem] * 3 + [hbm] * 2 + [anywhere] * 2 + [hbm] * 2,
        out_specs=(vmem, vmem),
        scratch_shapes=[
            pltpu.VMEM((2, rows, span), BF16),
            pltpu.VMEM((2 * before.shape[0], span), BF16),
            pltpu.VMEM((2, table_tiles, 256, TILE), BF16),
            pltpu.VMEM((ccds, 3, width), F32),
            pltpu.VMEM((2, tiles + 4, rows, TILE), BF16),
            pltpu.VMEM((ccds, (tiles + 2) * 32, TILE), BF16),
            pltpu.VMEM((ccds, tiles * 32, TILE), F32),
            pltpu.SemaphoreType.DMA((10,)),
        ],
        compiler_params=pltpu.CompilerParams(vmem_limit_bytes=VMEM_LIMIT),
        cost_estimate=HINT,
    )(pick, main, edge, bands, images, variances, before, after, col_warp, coeff)


def ends_kernel(images_hbm, variances_hbm, tails_ref, heads_ref, pixels, sems):
    _, rows, columns = pixels.shape
    step = columns // 4
    copies = []
    for p in range(4):
        cols = pl.ds(p * step, step)
        for kind, source in enumerate((images_hbm, variances_hbm)):
            copies.append(
                pltpu.make_async_copy(
                    source.at[:, cols], pixels.at[kind, :, cols], sems.at[2 * p + kind]
                )
            )
    for copy in copies:
        copy.start()
    out = lax.broadcasted_iota(jnp.int32, (48, rows), 0)
    tail = jnp.where(out < 24, 1, 0)
    out = out - jnp.where(out < 24, 0, 24)
    at = lax.broadcasted_iota(jnp.int32, (48, rows), 1)
    row = (out >> 3) + 29 * tail
    select = as_ones(((at >> 5) == (out & 7)) & ((at & 31) == row))
    for p in range(4):
        cols = slice(p * step, (p + 1) * step)
        parts = []
        for kind in range(2):
            copies[2 * p + kind].wait()
            parts.append(dot(select, pixels[kind, :, cols]))
        tails_ref[:, cols] = jnp.concatenate([part[:24] for part in parts], axis=0).astype(BF16)
        heads_ref[:, cols] = jnp.concatenate([part[24:] for part in parts], axis=0).astype(BF16)


def strip_ends(images, variances):
    rows, columns = images.shape
    out = jax.ShapeDtypeStruct((48, columns), BF16)
    vmem = pl.BlockSpec(memory_space=pltpu.VMEM)
    return pl.pallas_call(
        ends_kernel,
        out_shape=(out, out),
        in_specs=[pl.BlockSpec(memory_space=pltpu.HBM)] * 2,
        out_specs=(vmem, vmem),
        scratch_shapes=[pltpu.VMEM((2, rows, columns), BF16), pltpu.SemaphoreType.DMA((8,))],
        compiler_params=pltpu.CompilerParams(vmem_limit_bytes=VMEM_LIMIT),
        cost_estimate=HINT,
    )(images, variances)


def pieces_of(width, cuts=(), step=512):
    edges = sorted({0, width, *(cut for cut in cuts if 0 < cut < width)})
    pieces = []
    for low, high in zip(edges, edges[1:]):
        pieces += [(at, min(at + step, high)) for at in range(low, high, step)]
    return pieces


def stacked(refs, cols):
    return jnp.concatenate([ref[:, cols] for ref in refs], axis=0)


def first_kernel(two_ref, one_ref, three_ref, *refs):
    up_ref, down_ref = refs[4:]
    width = up_ref.shape[1]
    half = two_ref.shape[0]
    for side_ref, base in ((three_ref, 0), (one_ref, width)):
        select = jnp.concatenate([two_ref[...], side_ref[...]], axis=0)
        for low, high in pieces_of(width):
            out = dot(select, stacked(refs[:4], slice(base + low, base + high))).astype(BF16)
            if base == 0:
                up_ref[:half, low:high] = out[:half]
                down_ref[half:, low:high] = out[half:]
            else:
                down_ref[:half, low:high] = out[:half]
                up_ref[half:, low:high] = out[half:]


def second_kernel(one_ref, three_ref, own_select_ref, *refs):
    up_ref, down_ref, own_ref = refs[4:]
    width = up_ref.shape[1]
    half = one_ref.shape[0]
    for side_ref, base, out_ref in ((one_ref, 0, up_ref), (three_ref, width, down_ref)):
        select = jnp.concatenate([side_ref[...], own_select_ref[...]], axis=0)
        for low, high in pieces_of(width):
            out = dot(select, stacked(refs[:4], slice(base + low, base + high))).astype(BF16)
            out_ref[:, low:high] = out[:half]
            own_ref[:, base + low : base + high] = out[half:]


def first_sums(selects, sources, ahead):
    shape = (2 * selects[0].shape[0], sources[0].shape[1] // 2)
    return vmem_call(first_kernel, [(shape, BF16)] * 2, [*selects, *sources], ahead)


def second_sums(selects, sources, ahead):
    rows, width = selects[0].shape[0], sources[0].shape[1]
    shapes = [(rows, width // 2), (rows, width // 2), (rows, width)]
    shapes = [(shape, BF16) for shape in shapes]
    return vmem_call(second_kernel, shapes, [*selects, *sources], ahead)


def total(*terms):
    result = terms[0].astype(F32)
    for term in terms[1:]:
        result = result + term.astype(F32)
    return result


def passing_kernel(up_ref, down_ref, last_ref, next_ref, up_out, down_out):
    rows, width = up_ref.shape
    for low, high in pieces_of(width, step=256):
        cols = slice(low, high)
        up_out[:, cols] = total(up_ref[:, cols], last_ref[:rows, cols]).astype(BF16)
        down_out[:, cols] = total(down_ref[:, cols], next_ref[:rows, cols]).astype(BF16)


def passing_sums(up, down, from_last, from_next, ahead):
    shapes = [(up.shape, BF16), (down.shape, BF16)]
    return vmem_call(passing_kernel, shapes, [up, down, from_last, from_next], ahead)


def own_kernel(own_ref, last_ref, next_ref, flux_ref, weight_ref, kept_ref, *rest_refs):
    rows, width = flux_ref.shape
    strip = kept_ref.shape[0]
    for low, high in pieces_of(width, step=256):
        cols, right = slice(low, high), slice(width + low, width + high)
        flux = total(own_ref[:, cols], next_ref[rows:, cols], flux_ref[:, cols])
        weight = total(own_ref[:, right], last_ref[rows:, cols], weight_ref[:, cols])
        for at, values in ((cols, flux), (right, weight)):
            kept_ref[:, at] = values[:strip]
            for k, rest_ref in enumerate(rest_refs):
                rest_ref[:, at] = values[(k + 1) * strip : (k + 2) * strip].astype(BF16)


def own_sums(own, from_last, from_next, flux, weight, ahead):
    shape = (own.shape[0] // SIDE, own.shape[1])
    shapes = [(shape, F32)] + [(shape, BF16)] * 3
    return vmem_call(own_kernel, shapes, [own, from_last, from_next, flux, weight], ahead)


def coadd_kernel(kept_ref, one_ref, two_ref, three_ref, out_ref):
    width = out_ref.shape[1]
    terms = kept_ref, one_ref, two_ref, three_ref
    for low, high in pieces_of(width, step=256):
        numerator = total(*[ref[:, low:high] for ref in terms])
        denominator = total(*[ref[:, width + low : width + high] for ref in terms])
        out_ref[:, low:high] = (numerator / (1.0 + denominator)).astype(BF16)


def coadded(kept, arrived, ahead):
    shape = (kept.shape[0], kept.shape[1] // 2)
    return vmem_call(coadd_kernel, [(shape, BF16)], [kept, *arrived], ahead)[0]


def join_kernel(*refs):
    rows = refs[0].shape[0]
    for n, out_ref in enumerate(refs[2 * SIDE :]):
        for k in range(SIDE):
            out_ref[k * rows : (k + 1) * rows] = refs[SIDE * n + k][...]


def joined(blocks, ahead):
    shapes = [((SIDE * parts[0].shape[0], parts[0].shape[1]), BF16) for parts in blocks]
    return vmem_call(join_kernel, shapes, [part for parts in blocks for part in parts], ahead)


def patch_pieces(first, middle, columns, patch_refs):
    own_ref, next_ref, last_ref, left_ref, right_ref = patch_refs
    width, half = own_ref.shape[1], left_ref.shape[1]
    for low, high in pieces_of(width, (half, middle - first)):
        far_ref, base = (left_ref, 0) if high <= half else (right_ref, half)
        cols = slice(low, high)
        stack = [ref[:, cols] for ref in (own_ref, next_ref, last_ref)]
        stack.append(far_ref[:, low - base : high - base])
        yield low, high, 0 if first + high <= middle else 1, jnp.concatenate(stack, axis=0)


def lend_kernel(first, middle, columns, left_select, right_select, *refs):
    down_ref, up_ref = refs[5:]
    half = down_ref.shape[0]
    for low, high, side, stack in patch_pieces(first, middle, columns, refs[:5]):
        out = dot((left_select, right_select)[side][...], stack).astype(BF16)
        down_ref[:, low:high] = out[:half]
        up_ref[:, low:high] = out[half:]


def lent_rows(first, columns, selects, patches, ahead):
    shape = (selects[0].shape[0] // 2, patches[0].shape[1])
    kernel = functools.partial(lend_kernel, first, columns // 2, columns)
    return vmem_call(kernel, [(shape, BF16)] * 2, [*selects, *patches], ahead)


def difference_kernel(first, middle, columns, left_select, right_select, *refs):
    new_hbm, down_ref, up_ref = refs[5:8]
    out_hbm, new, result, sems = refs[-4:]
    count = new.shape[0]
    whole = patch_pieces(first, middle, columns, refs[:5])
    load = pltpu.make_async_copy(
        new_hbm.at[:, :, pl.ds(first, new.shape[2])], new, sems.at[0]
    )
    load.start()
    stores = []
    for p, (low, high, side, stack) in enumerate(whole):
        own = dot((left_select, right_select)[side][...], stack)
        cols = slice(low, high)
        if p == 0:
            load.wait()
        for c in range(count):
            here = slice(c * HALF, (c + 1) * HALF)
            there = slice((count + c) * HALF, (count + c + 1) * HALF)
            lower = own[here] + down_ref[here, cols].astype(F32)
            upper = own[there] + up_ref[here, cols].astype(F32)
            result[c, 0:HALF, cols] = (new[c, 0:HALF, cols].astype(F32) - lower).astype(BF16)
            result[c, HALF : 2 * HALF, cols] = (
                new[c, HALF : 2 * HALF, cols].astype(F32) - upper
            ).astype(BF16)
        store = pltpu.make_async_copy(
            result.at[:, :, pl.ds(low, high - low)],
            out_hbm.at[:, :, pl.ds(first + low, high - low)],
            sems.at[1 + p],
        )
        store.start()
        stores.append(store)
    for store in stores:
        store.wait()


def difference_block(first, selects, patches, new_images, down, up, running):
    width, half = patches[0].shape[1], patches[3].shape[1]
    rows, depth = selects[0].shape
    count, strip_rows, columns = new_images.shape
    vmem = pl.BlockSpec(memory_space=pltpu.VMEM)
    hbm = pl.BlockSpec(memory_space=pltpu.HBM)
    operands = [*selects, *patches, new_images, down, up]
    specs = [vmem] * 7 + [pl.BlockSpec(memory_space=pl.ANY)] + [vmem] * 2
    aliases = {}
    if running is not None:
        aliases = {len(operands): 0}
        operands.append(running)
        specs.append(hbm)
    count_pieces = len(pieces_of(width, (half, columns // 2 - first)))
    block = pltpu.VMEM((count, strip_rows, width), BF16)
    return pl.pallas_call(
        functools.partial(difference_kernel, first, columns // 2, columns),
        out_shape=jax.ShapeDtypeStruct(new_images.shape, BF16),
        in_specs=specs,
        out_specs=hbm,
        scratch_shapes=[block, block, pltpu.SemaphoreType.DMA((1 + count_pieces,))],
        input_output_aliases=aliases,
        compiler_params=pltpu.CompilerParams(vmem_limit_bytes=VMEM_LIMIT),
        cost_estimate=HINT,
    )(*operands)


def ring_step(index, table):
    value = jnp.full_like(index, table[3])
    for k in range(3):
        value = jnp.where(index == k, table[k], value)
    return value


def patch_keys(shape, axis, table, x_first, position):
    at = lax.broadcasted_iota(jnp.int32, shape, axis)
    outer, inner = ring_step(at >> 7, table), (at >> 5) & 3
    dx, dy = (outer, inner) if x_first else (inner, outer)
    base_y, base_x = position >> 2, position & 3
    name = (((base_y + dy) & 3) << 2) + ((base_x + dx) & 3)
    return (name << 8) + HALF + (at & 31)


def ccd_keys(shape, axis, source, k, patch_ref, offset_ref):
    at = lax.broadcasted_iota(jnp.int32, shape, axis)
    ccd, row = at >> 4, at & 15
    key = row + (0, HALF, 2 * HALF, -HALF)[source]
    for c in range(8):
        known = (patch_ref[c, k] << 8) + offset_ref[c, k]
        key = key + jnp.where(ccd == c, known, 0)
    return key


def as_ones(mask):
    return jnp.where(mask, 1.0, 0.0).astype(BF16)


def matrices_kernel(
    position_ref,
    send_patch,
    send_offset,
    request_patch,
    request_offset,
    warp_ref,
    taps_ref,
    main_ref,
    edge_ref,
    bands_ref,
    *select_refs,
):
    position = position_ref[0]
    rows, reach = warp_ref.shape
    at = lax.broadcasted_iota(jnp.int32, (reach, rows), 1)
    tap = lax.broadcasted_iota(jnp.int32, (reach, rows), 0)
    spread = as_ones(tap == (at & 31) + 3)
    own = lax.broadcasted_iota(jnp.int32, (rows, rows), 0) >> 5
    same = own == lax.broadcasted_iota(jnp.int32, (rows, rows), 1) >> 5
    at = lax.broadcasted_iota(jnp.int32, (reach, 96), 1)
    tap = lax.broadcasted_iota(jnp.int32, (reach, 96), 0)
    place = at - jnp.where(at >= 48, 48, 0)
    place = place - jnp.where(place >= 24, 24, 0)
    edge_spread = as_ones(tap == (place >> 3) + jnp.where(at >= 48, 35, 0))
    at = lax.broadcasted_iota(jnp.int32, (rows, 96), 1)
    at = at - jnp.where(at >= 48, 48, 0)
    kinds = jnp.where(at >= 24, 1, 0)
    at = at - 24 * kinds
    edge_same = (lax.broadcasted_iota(jnp.int32, (rows, 96), 0) >> 5) == (at & 7)
    warp = warp_ref[...]
    for kind, matrix in enumerate((warp, squared(warp))):
        main_ref[kind] = jnp.where(same, dot(matrix, spread), 0.0).astype(BF16)
        kept = edge_same & (kinds == kind)
        edge_ref[kind] = jnp.where(kept, dot(matrix, edge_spread), 0.0).astype(BF16)
    source = lax.broadcasted_iota(jnp.int32, (TILE, TILE), 0)
    target = lax.broadcasted_iota(jnp.int32, (TILE, TILE), 1)
    near = jnp.abs(source - target) < 64
    for c in range(bands_ref.shape[0]):
        for b in range(3):
            row = jnp.broadcast_to(taps_ref[3 * c + b : 3 * c + b + 1], (TILE, TILE))
            turned = pltpu.roll(row, 0, 1, stride=1, stride_axis=0)
            cols = slice(b * TILE, (b + 1) * TILE)
            bands_ref[c, 0:TILE, cols] = jnp.where(near, turned, 0.0).astype(BF16)
            bands_ref[c, TILE : 2 * TILE, cols] = jnp.where(near, 0.0, turned).astype(BF16)
    for j in range(2):
        sums_refs = select_refs[4 * j : 4 * j + 4]
        keys = patch_keys((512, TILE), 0, (2, 1, 3, 0), j == 0, position)
        for source in range(4):
            hit = None
            for k in range(2):
                key = ccd_keys((1, TILE), 1, source, k, send_patch, send_offset)
                hit = keys == key if hit is None else hit | (keys == key)
            block = as_ones(hit)
            cols = slice(source * TILE, (source + 1) * TILE)
            for q, ref in enumerate(sums_refs):
                ref[:, cols] = block[q * TILE : (q + 1) * TILE]
    for n, (j, h) in enumerate(((0, 0), (0, 1), (1, 1))):
        own_ref, lent_ref = select_refs[8 + 2 * n : 10 + 2 * n]
        keys = patch_keys((1, 512), 1, (0, 1, 3, 2), j == 0, position)
        for source in range(4):
            key = ccd_keys((TILE, TILE), 0, source, h, request_patch, request_offset)
            out_ref = (own_ref, lent_ref)[source // 2]
            place = slice(source % 2 * TILE, (source % 2 + 1) * TILE)
            for q in range(4):
                cols = slice(q * TILE, (q + 1) * TILE)
                out_ref[place, cols] = as_ones(key == keys[:, cols])


def matrices(position, send_patch, send_offset, request_patch, request_offset, row_warp, kernels):
    count, rows, reach = row_warp.shape
    flat = count * rows
    taps = kernels.shape[-1]
    turned = kernels.astype(F32).reshape(count * 3, taps)[:, ::-1]
    reachout = taps // 2
    turned = jnp.concatenate(
        [
            turned[:, reachout:],
            jnp.zeros((count * 3, TILE - taps), F32),
            turned[:, :reachout],
        ],
        axis=1,
    )
    smem = pl.BlockSpec(memory_space=pltpu.SMEM)
    vmem = pl.BlockSpec(memory_space=pltpu.VMEM)
    heights = [TILE] * 8 + [2 * TILE] * 6
    shapes = [(2, flat, flat), (2, flat, 96), (count, 256, 3 * TILE)]
    shapes += [(height, 4 * TILE) for height in heights]
    return pl.pallas_call(
        matrices_kernel,
        out_shape=[jax.ShapeDtypeStruct(shape, BF16) for shape in shapes],
        in_specs=[smem] * 5 + [vmem] * 2,
        out_specs=[vmem] * len(shapes),
        compiler_params=pltpu.CompilerParams(vmem_limit_bytes=VMEM_LIMIT),
        cost_estimate=HINT,
    )(
        position.reshape(1),
        send_patch,
        send_offset,
        request_patch,
        request_offset,
        row_warp.reshape(flat, reach),
        turned,
    )


def body(
    images,
    variances,
    row_warp,
    col_warp,
    warp_index,
    psf_kernels,
    psf_coeff,
    send_patch,
    send_offset,
    request_patch,
    request_offset,
    new_images,
):
    count, rows, columns = images.shape
    flat = count * rows
    blocks = list(zip(BOUNDS, BOUNDS[1:]))
    position = lax.axis_index("ccd")

    plain = images.reshape(flat, columns), variances.reshape(flat, columns)
    plain, col_warp, psf_coeff = jax.tree.map(in_hbm, (plain, col_warp, psf_coeff))
    tails, heads = strip_ends(*plain)
    before = strip_shift(tails, 1, wrap=False)
    after = strip_shift(heads, -1, wrap=False)
    main, edge, bands, *selects = matrices(
        position, send_patch, send_offset, request_patch, request_offset, row_warp, psf_kernels
    )
    axes = [("x", "y"), ("y", "x")]

    sources = []
    for first, last in blocks:
        low, high = ccd_block(
            first,
            last - first,
            warp_index[:, 0],
            main,
            edge,
            bands,
            *plain,
            before,
            after,
            col_warp,
            psf_coeff,
        )
        sources.append((low, high, strip_shift(low, -1), strip_shift(high, 1)))

    steps = range(len(blocks))
    queue = [sources[-1][:1]]

    def ordered(function, *operands):
        result = function(*operands, queue[-1])
        queue.append([result[0]] if isinstance(result, (list, tuple)) else [result])
        return result

    sums, second, passed = [], [], []
    for j in steps:
        two, one, three, zero = selects[4 * j : 4 * j + 4]
        up, down = ordered(first_sums, (two, one, three), sources[j])
        sums.append((plane_shift(up, axes[j][0], 1), plane_shift(down, axes[j][0], -1)))
        second.append(ordered(second_sums, (one, three, zero), sources[j]))
    for j in steps:
        up, down = ordered(passing_sums, *second[j][:2], *sums[j])
        passed.append((plane_shift(up, axes[j][0], 1), plane_shift(down, axes[j][0], -1)))
    spread = []
    for j in steps:
        axis = axes[j][1]
        kept, one, two, three = ordered(own_sums, second[j][2], *sums[j], *passed[j])
        two, one, three = [
            plane_shift(value, axis, shift) for value, shift in ((two, 2), (one, 1), (three, -1))
        ]
        spread.append((kept, (one, two, three)))
    coadds, shared = [], []
    for j in steps:
        coadds.append(ordered(coadded, *spread[j]))
        shared.append([plane_shift(coadds[j], axes[j][1], shift) for shift in (-1, 2, 1)])
    window = jnp.concatenate(coadds, axis=1)
    lower = strip_shift(window[HALF:], 1)
    held = []
    for j, block in enumerate(ordered(joined, [[coadds[j], *shared[j]] for j in steps])):
        held.append((block, plane_shift(block, axes[j][0], -1), plane_shift(block, axes[j][0], 1)))
    queue[-1] = queue[-1] + [lower]
    gathered = {}
    for j in steps:
        axis = axes[j][0]
        block, following, last = held[j]
        half = block.shape[1] // 2
        left = plane_shift(last[:, :half], axis, 1)
        right = plane_shift(following[:, half:], axis, -1)
        gathered[j] = block, following, last, left, right
    lent = {}
    for j in steps:
        asks = selects[8:12] if j == 0 else selects[12:] * 2
        down, up = ordered(lent_rows, blocks[j][0], columns, asks[1::2], gathered[j])
        lent[j] = asks[::2], strip_shift(down, 1), strip_shift(up, -1)
    patch_coadd = jnp.concatenate([lower, window[:HALF]], axis=0)
    difference = None
    for j in steps:
        asks, down, up = lent[j]
        difference = difference_block(
            blocks[j][0], asks, gathered[j], new_images, down, up, difference
        )

    return (patch_coadd[None], difference)


def solution(mesh):
    return jax.shard_map(
        body,
        mesh=mesh,
        in_specs=(
            P("ccd", "strip", None),
            P("ccd", "strip", None),
            P("ccd", "strip", None),
            P(),
            P("ccd", "strip"),
            P("ccd", None, None),
            P("ccd", "strip", None, None),
            P("ccd", None),
            P("ccd", None),
            P("ccd", None),
            P("ccd", None),
            P("ccd", "strip", None),
        ),
        out_specs=(P("ccd", "strip", None), P("ccd", "strip", None)),
        check_vma=False,
    )
```

```python
import functools

import jax
import jax.numpy as jnp
from jax import lax
from jax.experimental import pallas as pl
from jax.experimental.pallas import tpu as pltpu
from jax.sharding import PartitionSpec as P

TILE = 128
SIDE = 4
HALF = 16
BOUNDS = (0, 2304, 4096)
F32 = jnp.float32
BF16 = jnp.bfloat16
MIB = 1024 * 1024


def strip_shift(value, steps, wrap=True):
    count = lax.axis_size("strip")
    pairs = [(i, (i + steps) % count) for i in range(count) if wrap or 0 <= i + steps < count]
    return lax.ppermute(value, "strip", pairs)


def plane_shift(value, axis, steps):
    pairs = []
    for i in range(SIDE * SIDE):
        y, x = divmod(i, SIDE)
        if axis == "x":
            x = (x + steps) % SIDE
        else:
            y = (y + steps) % SIDE
        pairs.append((i, y * SIDE + x))
    return lax.ppermute(value, "ccd", pairs)


def plane_swap(value, axis, mask):
    pairs = []
    for i in range(SIDE * SIDE):
        y, x = divmod(i, SIDE)
        pairs.append((i, y * SIDE + (x ^ mask) if axis == "x" else (y ^ mask) * SIDE + x))
    return lax.ppermute(value, "ccd", pairs)


def dot(a, b):
    return jnp.dot(a, b, preferred_element_type=F32)


def in_hbm(value):
    return pltpu.with_memory_space_constraint(value, pltpu.HBM)


def squared(values):
    wide = values.astype(F32)
    return (wide * wide).astype(BF16)


HINT = pl.CostEstimate(flops=1, bytes_accessed=1, transcendentals=0)


def vmem_call(kernel, shapes, operands, ahead=()):
    count = len(operands)

    def ordered(*refs):
        kernel(*refs[:count], *refs[count + len(ahead) :])

    vmem = pl.BlockSpec(memory_space=pltpu.VMEM)
    return pl.pallas_call(
        ordered,
        out_shape=[jax.ShapeDtypeStruct(shape, dtype) for shape, dtype in shapes],
        in_specs=[vmem] * count + [pl.BlockSpec(memory_space=pl.ANY)] * len(ahead),
        out_specs=[vmem] * len(shapes),
        compiler_params=pltpu.CompilerParams(vmem_limit_bytes=16 * MIB),
        cost_estimate=HINT,
    )(*operands, *ahead)


def ccd_kernel(
    first,
    width,
    columns,
    pick_ref,
    main_ref,
    edge_ref,
    bands_ref,
    images_hbm,
    variances_hbm,
    before_hbm,
    after_hbm,
    table_hbm,
    coeff_hbm,
    ahead_ref,
    low_ref,
    high_ref,
    pixels,
    rims,
    table,
    coeff,
    rowed,
    warped,
    inverse,
    sems,
):
    tiles = width // TILE
    all_tiles = columns // TILE
    t0 = first // TILE
    start = max(first - 2 * TILE, 0)
    stop = min(first + width + 2 * TILE, columns)
    span = stop - start
    table_start = max(t0 - 1, 0)
    table_stop = min(t0 + tiles + 1, all_tiles)
    rows = main_ref.shape[1]
    ccds = rows // 32
    edge_rows = before_hbm.shape[0]
    pieces = [(0, 768), (768, span - 768)]
    loads = []
    for p, (at, size) in enumerate(pieces):
        here, there = pl.ds(at, size), pl.ds(start + at, size)
        loads.append(
            [
                pltpu.make_async_copy(
                    images_hbm.at[:, there], pixels.at[0, :, here], sems.at[4 * p]
                ),
                pltpu.make_async_copy(
                    variances_hbm.at[:, there], pixels.at[1, :, here], sems.at[4 * p + 1]
                ),
                pltpu.make_async_copy(
                    before_hbm.at[:, there], rims.at[pl.ds(0, edge_rows), here], sems.at[4 * p + 2]
                ),
                pltpu.make_async_copy(
                    after_hbm.at[:, there],
                    rims.at[pl.ds(edge_rows, edge_rows), here],
                    sems.at[4 * p + 3],
                ),
            ]
        )
    load_table = pltpu.make_async_copy(
        table_hbm.at[:, pl.ds(table_start, table_stop - table_start), pl.ds(64, 256), :],
        table,
        sems.at[8],
    )
    load_coeff = pltpu.make_async_copy(
        coeff_hbm, coeff, sems.at[9]
    )
    for copy in loads[0] + loads[1] + [load_table, load_coeff]:
        copy.start()
    shift = (start - (first - 2 * TILE)) // TILE
    if shift > 0:
        rowed[:, 0:shift] = jnp.zeros((2, shift, rows, TILE), BF16)
    end = shift + span // TILE
    if end < tiles + 4:
        rowed[:, end : tiles + 4] = jnp.zeros((2, tiles + 4 - end, rows, TILE), BF16)
    for (at, size), copies in zip(pieces, loads):
        for copy in copies:
            copy.wait()
        for j in range(at // 256, (at + size) // 256):
            here = slice(j * 256, (j + 1) * 256)
            edges = rims[:, here]
            for kind in range(2):
                out = dot(main_ref[kind], pixels[kind, :, here]) + dot(edge_ref[kind], edges)
                out = out.astype(BF16)
                rowed[kind, shift + 2 * j] = out[:, :TILE]
                rowed[kind, shift + 2 * j + 1] = out[:, TILE:]
    load_table.wait()
    lane = lax.broadcasted_iota(jnp.int32, (rows, TILE), 1)

    def with_halo(own, previous, following):
        halo = jnp.where(lane[: own.shape[0]] < 64, following, previous)
        return jnp.concatenate([own, halo], axis=1)

    def weights(k):
        parts = []
        for m in range(2):
            part = table[m, k]
            parts.append(jnp.concatenate([part[64:192], part[192:256], part[0:64]], axis=0))
        return jnp.concatenate(parts, axis=1)

    def choose(product, c):
        block = product[c * 32 : (c + 1) * 32]
        return jnp.where(pick_ref[c] == 0, block[:, :TILE], block[:, TILE:])

    def column_step(w, with_variance):
        matrix = weights(w + (t0 - 1 - table_start))
        product = dot(with_halo(rowed[0, w + 1], rowed[0, w], rowed[0, w + 2]), matrix)
        at = pl.ds(pl.multiple_of(w * 32, 32), 32)
        for c in range(ccds):
            warped[c, at] = choose(product, c).astype(BF16)
        if with_variance:
            product = dot(
                with_halo(rowed[1, w + 1], rowed[1, w], rowed[1, w + 2]), squared(matrix)
            )
            at = pl.ds(pl.multiple_of((w - 1) * 32, 32), 32)
            for c in range(ccds):
                inverse[c, at] = 1.0 / choose(product, c)

    for w in (0, tiles + 1):
        if 0 <= t0 - 1 + w < all_tiles:
            column_step(w, False)
        else:
            warped[:, w * 32 : (w + 1) * 32] = jnp.zeros((ccds, 32, TILE), BF16)

    group = max(size for size in range(1, 9) if tiles % size == 0)

    def column_loop(w, carry):
        column_step(w, True)
        return carry

    lax.fori_loop(1, tiles + 1, column_loop, 0, unroll=tiles // 2)
    load_coeff.wait()

    def ccd_step(c, carry):
        row16 = pl.ds(pl.multiple_of(c * HALF, HALF), HALF)
        for g in range(tiles // group):
            base = g * group * 32
            size = group * 32
            own = warped[c, base + 32 : base + 32 + size]
            lhs = with_halo(
                own, warped[c, base : base + size], warped[c, base + 64 : base + 64 + size]
            )
            convolved = dot(lhs, bands_ref[c])
            for k in range(group):
                tile = g * group + k
                here = slice(k * 32, (k + 1) * 32)
                matched = own[here].astype(F32)
                for b in range(3):
                    factor = coeff[c, b, t0 + tile : t0 + tile + 1]
                    matched = matched + factor * convolved[here, b * TILE : (b + 1) * TILE]
                weight = inverse[c, tile * 32 : (tile + 1) * 32]
                flux = (matched * weight).astype(BF16)
                weight = weight.astype(BF16)
                left = slice(tile * TILE, (tile + 1) * TILE)
                right = slice(width + tile * TILE, width + (tile + 1) * TILE)
                low_ref[row16, left] = flux[:HALF]
                high_ref[row16, left] = flux[HALF:]
                low_ref[row16, right] = weight[:HALF]
                high_ref[row16, right] = weight[HALF:]
        return carry

    lax.fori_loop(0, ccds, ccd_step, 0, unroll=ccds)


def ccd_block(
    first, width, pick, main, edge, bands, images, variances, before, after, col_warp, coeff, ahead
):
    rows, columns = images.shape
    tiles = width // TILE
    span = min(first + width + 2 * TILE, columns) - max(first - 2 * TILE, 0)
    table_tiles = min(first // TILE + tiles + 1, columns // TILE) - max(first // TILE - 1, 0)
    ccds = rows // 32
    vmem = pl.BlockSpec(memory_space=pltpu.VMEM)
    anywhere = pl.BlockSpec(memory_space=pl.ANY)
    hbm = pl.BlockSpec(memory_space=pltpu.HBM)
    out = jax.ShapeDtypeStruct((rows // 2, 2 * width), BF16)
    return pl.pallas_call(
        functools.partial(ccd_kernel, first, width, columns),
        out_shape=(out, out),
        in_specs=[pl.BlockSpec(memory_space=pltpu.SMEM)] + [vmem] * 3 + [hbm] * 2 + [anywhere] * 2 + [hbm] * 2 + [anywhere],
        out_specs=(vmem, vmem),
        scratch_shapes=[
            pltpu.VMEM((2, rows, span), BF16),
            pltpu.VMEM((2 * before.shape[0], span), BF16),
            pltpu.VMEM((2, table_tiles, 256, TILE), BF16),
            pltpu.VMEM(coeff.shape, F32),
            pltpu.VMEM((2, tiles + 4, rows, TILE), BF16),
            pltpu.VMEM((ccds, (tiles + 2) * 32, TILE), BF16),
            pltpu.VMEM((ccds, tiles * 32, TILE), F32),
            pltpu.SemaphoreType.DMA((10,)),
        ],
        compiler_params=pltpu.CompilerParams(vmem_limit_bytes=24 * MIB),
        cost_estimate=HINT,
    )(pick, main, edge, bands, images, variances, before, after, col_warp, coeff, ahead[0])


def ends_kernel(images_hbm, variances_hbm, tails_ref, heads_ref, pixels, sems):
    _, rows, columns = pixels.shape
    step = columns // 4
    copies = []
    for p in range(4):
        cols = pl.ds(p * step, step)
        for kind, source in enumerate((images_hbm, variances_hbm)):
            copies.append(
                pltpu.make_async_copy(
                    source.at[:, cols], pixels.at[kind, :, cols], sems.at[2 * p + kind]
                )
            )
    for copy in copies:
        copy.start()
    for p in range(4):
        for kind in range(2):
            copies[2 * p + kind].wait()
        for low in range(p * step, (p + 1) * step, 256):
            cols = slice(low, low + 256)
            tails, heads = [], []
            for kind in range(2):
                for c in range(rows // 32):
                    tail = pixels[kind, c * 32 + 16 : c * 32 + 32, cols].astype(F32)
                    tails.append(tail[13:])
                    heads.append(pixels[kind, c * 32 : c * 32 + 16, cols].astype(F32)[:3])
            tails_ref[:, cols] = jnp.concatenate(tails, axis=0).astype(BF16)
            heads_ref[:, cols] = jnp.concatenate(heads, axis=0).astype(BF16)


def strip_ends(images, variances):
    rows, columns = images.shape
    out = jax.ShapeDtypeStruct((48, columns), BF16)
    vmem = pl.BlockSpec(memory_space=pltpu.VMEM)
    return pl.pallas_call(
        ends_kernel,
        out_shape=(out, out),
        in_specs=[pl.BlockSpec(memory_space=pltpu.HBM)] * 2,
        out_specs=(vmem, vmem),
        scratch_shapes=[pltpu.VMEM((2, rows, columns), BF16), pltpu.SemaphoreType.DMA((8,))],
        compiler_params=pltpu.CompilerParams(vmem_limit_bytes=8 * MIB),
        cost_estimate=HINT,
    )(images, variances)


def pieces_of(width, cuts=(), step=512):
    edges = sorted({0, width, *(cut for cut in cuts if 0 < cut < width)})
    pieces = []
    for low, high in zip(edges, edges[1:]):
        pieces += [(at, min(at + step, high)) for at in range(low, high, step)]
    return pieces


def stacked(refs, cols):
    return jnp.concatenate([ref[:, cols] for ref in refs], axis=0)


def first_kernel(two_ref, one_ref, three_ref, *refs):
    up_ref, down_ref = refs[4:]
    width = up_ref.shape[1]
    half = two_ref.shape[0]
    for side_ref, base in ((three_ref, 0), (one_ref, width)):
        select = jnp.concatenate([two_ref[...], side_ref[...]], axis=0)
        for low, high in pieces_of(width):
            out = dot(select, stacked(refs[:4], slice(base + low, base + high))).astype(BF16)
            if base == 0:
                up_ref[:half, low:high] = out[:half]
                down_ref[half:, low:high] = out[half:]
            else:
                down_ref[:half, low:high] = out[:half]
                up_ref[half:, low:high] = out[half:]


def second_kernel(one_ref, three_ref, own_select_ref, *refs):
    up_ref, down_ref, own_ref = refs[4:]
    width = up_ref.shape[1]
    half = one_ref.shape[0]
    for side_ref, base, out_ref in ((one_ref, 0, up_ref), (three_ref, width, down_ref)):
        select = jnp.concatenate([side_ref[...], own_select_ref[...]], axis=0)
        for low, high in pieces_of(width):
            out = dot(select, stacked(refs[:4], slice(base + low, base + high))).astype(BF16)
            out_ref[:, low:high] = out[:half]
            own_ref[:, base + low : base + high] = out[half:]


def first_sums(selects, sources, ahead):
    shape = (2 * selects[0].shape[0], sources[0].shape[1] // 2)
    return vmem_call(first_kernel, [(shape, BF16)] * 2, [*selects, *sources], ahead)


def second_sums(selects, sources, ahead):
    rows, width = selects[0].shape[0], sources[0].shape[1]
    shapes = [(rows, width // 2), (rows, width // 2), (rows, width)]
    shapes = [(shape, BF16) for shape in shapes]
    return vmem_call(second_kernel, shapes, [*selects, *sources], ahead)


def total(*terms):
    result = terms[0].astype(F32)
    for term in terms[1:]:
        result = result + term.astype(F32)
    return result


def passing_kernel(up_ref, down_ref, last_ref, next_ref, up_out, down_out):
    rows, width = up_ref.shape
    for low, high in pieces_of(width, step=256):
        cols = slice(low, high)
        up_out[:, cols] = total(up_ref[:, cols], last_ref[:rows, cols]).astype(BF16)
        down_out[:, cols] = total(down_ref[:, cols], next_ref[:rows, cols]).astype(BF16)


def passing_sums(up, down, from_last, from_next, ahead):
    shapes = [(up.shape, BF16), (down.shape, BF16)]
    return vmem_call(passing_kernel, shapes, [up, down, from_last, from_next], ahead)


def own_kernel(own_ref, last_ref, next_ref, flux_ref, weight_ref, kept_ref, *rest_refs):
    rows, width = flux_ref.shape
    strip = kept_ref.shape[0]
    for low, high in pieces_of(width, step=256):
        cols, right = slice(low, high), slice(width + low, width + high)
        flux = total(own_ref[:, cols], next_ref[rows:, cols], flux_ref[:, cols])
        weight = total(own_ref[:, right], last_ref[rows:, cols], weight_ref[:, cols])
        for at, values in ((cols, flux), (right, weight)):
            kept_ref[:, at] = values[:strip]
            for k, rest_ref in enumerate(rest_refs):
                rest_ref[:, at] = values[(k + 1) * strip : (k + 2) * strip].astype(BF16)


def own_sums(own, from_last, from_next, flux, weight, ahead):
    shape = (own.shape[0] // SIDE, own.shape[1])
    shapes = [(shape, F32)] + [(shape, BF16)] * 3
    return vmem_call(own_kernel, shapes, [own, from_last, from_next, flux, weight], ahead)


def coadd_kernel(*refs):
    terms, (left_ref, rest_ref) = refs[:4], refs[4:]
    width, middle = terms[0].shape[1] // 2, left_ref.shape[1]
    for low, high in pieces_of(width, (middle,), step=256):
        numerator = total(*[ref[:, low:high] for ref in terms])
        denominator = total(*[ref[:, width + low : width + high] for ref in terms])
        result = (numerator / (1.0 + denominator)).astype(BF16)
        if high <= middle:
            left_ref[:, low:high] = result
        else:
            rest_ref[:, low - middle : high - middle] = result


def later_coadd_kernel(*refs):
    terms, (rest_ref, right_ref) = refs[:4], refs[4:]
    width, base = terms[0].shape[1] // 2, rest_ref.shape[1]
    right_ref[:, :base] = rest_ref[...]
    for low, high in pieces_of(width, step=256):
        numerator = total(*[ref[:, low:high] for ref in terms])
        denominator = total(*[ref[:, width + low : width + high] for ref in terms])
        right_ref[:, base + low : base + high] = (numerator / (1.0 + denominator)).astype(BF16)


def coadded(kept, arrived, half, ahead):
    rows = kept.shape[0]
    shapes = [((rows, half), BF16), ((rows, kept.shape[1] // 2 - half), BF16)]
    return vmem_call(coadd_kernel, shapes, [kept, *arrived], ahead)


def later_coadded(kept, arrived, rest, ahead):
    shape = (kept.shape[0], kept.shape[1] // 2 + rest.shape[1])
    return vmem_call(later_coadd_kernel, [(shape, BF16)], [kept, *arrived, rest], ahead)[0]


def join_kernel(*refs):
    count = len(refs) // 3
    for first_ref, second_ref, out_ref in zip(refs[::2], refs[1::2], refs[2 * count :]):
        rows = first_ref.shape[0]
        out_ref[:rows] = first_ref[...]
        out_ref[rows:] = second_ref[...]


def joined(pairs, ahead):
    shapes = [((2 * first.shape[0], first.shape[1]), BF16) for first, _ in pairs]
    return vmem_call(join_kernel, shapes, [value for pair in pairs for value in pair], ahead)


def patch_pieces(patch_refs):
    own_ref, next_ref, last_ref, left_ref, right_ref = patch_refs
    width, half = own_ref.shape[1], left_ref.shape[1]
    for low, high in pieces_of(width, (half,)):
        far_ref, base = (left_ref, 0) if high <= half else (right_ref, half)
        cols = slice(low, high)
        stack = [ref[:, cols] for ref in (own_ref, next_ref, last_ref)]
        stack.append(far_ref[:, low - base : high - base])
        yield low, high, jnp.concatenate(stack, axis=0)


def lend_kernel(select_ref, *refs):
    down_ref, up_ref = refs[5:]
    half = up_ref.shape[0] - HALF
    for ref in (down_ref, up_ref):
        ref[half:] = refs[0][HALF : 2 * HALF]
    for low, high, stack in patch_pieces(refs[:5]):
        out = dot(select_ref[...], stack).astype(BF16)
        down_ref[:half, low:high] = out[:half]
        up_ref[:half, low:high] = out[half:]


def lent_rows(select, patches, ahead):
    rows, width = select.shape[0] // 2, patches[0].shape[1]
    shapes = [((rows + HALF, width), BF16)] * 2
    return vmem_call(lend_kernel, shapes, [select, *patches], ahead)


def difference_kernel(first, select_ref, *refs):
    new_hbm, down_ref, up_ref = refs[5:8]
    out_hbm, coadd_hbm, new, result, coadd, sems = refs[-6:]
    count, _, width = new.shape
    here = pl.ds(first, width)
    coadd[:HALF] = down_ref[count * HALF :]
    coadd[HALF:] = refs[0][:HALF]
    store_coadd = pltpu.make_async_copy(coadd, coadd_hbm.at[:, here], sems.at[1])
    store_coadd.start()
    load = pltpu.make_async_copy(new_hbm.at[:, :, here], new, sems.at[0])
    load.start()
    stores = [store_coadd]
    for p, (low, high, stack) in enumerate(patch_pieces(refs[:5])):
        own = dot(select_ref[...], stack)
        cols = slice(low, high)
        if p == 0:
            load.wait()
        for c in range(count):
            here = slice(c * HALF, (c + 1) * HALF)
            there = slice((count + c) * HALF, (count + c + 1) * HALF)
            lower = own[here] + down_ref[here, cols].astype(F32)
            upper = own[there] + up_ref[here, cols].astype(F32)
            result[c, 0:HALF, cols] = (new[c, 0:HALF, cols].astype(F32) - lower).astype(BF16)
            result[c, HALF : 2 * HALF, cols] = (
                new[c, HALF : 2 * HALF, cols].astype(F32) - upper
            ).astype(BF16)
        store = pltpu.make_async_copy(
            result.at[:, :, pl.ds(low, high - low)],
            out_hbm.at[:, :, pl.ds(first + low, high - low)],
            sems.at[2 + p],
        )
        store.start()
        stores.append(store)
    for store in stores:
        store.wait()


def difference_block(first, select, patches, new_images, down, up, running):
    width, half = patches[0].shape[1], patches[3].shape[1]
    count, strip_rows, columns = new_images.shape
    vmem = pl.BlockSpec(memory_space=pltpu.VMEM)
    hbm = pl.BlockSpec(memory_space=pltpu.HBM)
    operands = [select, *patches, new_images, down, up]
    specs = [vmem] * 6 + [pl.BlockSpec(memory_space=pl.ANY)] + [vmem] * 2
    aliases = {}
    if running is not None:
        aliases = {len(operands): 0, len(operands) + 1: 1}
        operands += running
        specs += [hbm, hbm]
    count_pieces = len(pieces_of(width, (half,)))
    block = pltpu.VMEM((count, strip_rows, width), BF16)
    return pl.pallas_call(
        functools.partial(difference_kernel, first),
        out_shape=[
            jax.ShapeDtypeStruct(new_images.shape, BF16),
            jax.ShapeDtypeStruct((strip_rows, columns), BF16),
        ],
        in_specs=specs,
        out_specs=[hbm, hbm],
        scratch_shapes=[
            block,
            block,
            pltpu.VMEM((strip_rows, width), BF16),
            pltpu.SemaphoreType.DMA((2 + count_pieces,)),
        ],
        input_output_aliases=aliases,
        compiler_params=pltpu.CompilerParams(vmem_limit_bytes=16 * MIB),
        cost_estimate=HINT,
    )(*operands)


def ring_step(index, table):
    value = jnp.full_like(index, table[3])
    for k in range(3):
        value = jnp.where(index == k, table[k], value)
    return value


def patch_keys(shape, axis, table, x_first, swapped, position):
    at = lax.broadcasted_iota(jnp.int32, shape, axis)
    outer, inner = ring_step(at >> 7, table), (at >> 5) & 3
    base = position >> 2, position & 3
    outer_base, inner_base = base[::-1] if x_first else base
    outer = (outer_base + outer) & 3
    inner = inner_base ^ inner ^ (inner >> 1) if swapped else (inner_base + inner) & 3
    y, x = (inner, outer) if x_first else (outer, inner)
    name = (y << 2) + x
    return (name << 8) + HALF + (at & 31)


def ccd_keys(shape, axis, source, k, patch_ref, offset_ref):
    at = lax.broadcasted_iota(jnp.int32, shape, axis)
    ccd, row = at >> 4, at & 15
    key = row + (0, HALF, 2 * HALF, -HALF)[source]
    for c in range(8):
        known = (patch_ref[c, k] << 8) + offset_ref[c, k]
        key = key + jnp.where(ccd == c, known, 0)
    return key


def as_ones(mask):
    return jnp.where(mask, 1.0, 0.0).astype(BF16)


def matrices_kernel(warp_ref, taps_ref, main_ref, edge_ref, bands_ref):
    rows, reach = warp_ref.shape
    at = lax.broadcasted_iota(jnp.int32, (reach, rows), 1)
    tap = lax.broadcasted_iota(jnp.int32, (reach, rows), 0)
    spread = as_ones(tap == (at & 31) + 3)
    own = lax.broadcasted_iota(jnp.int32, (rows, rows), 0) >> 5
    same = own == lax.broadcasted_iota(jnp.int32, (rows, rows), 1) >> 5
    at = lax.broadcasted_iota(jnp.int32, (reach, 96), 1)
    tap = lax.broadcasted_iota(jnp.int32, (reach, 96), 0)
    place = at - jnp.where(at >= 48, 48, 0)
    place = place - jnp.where(place >= 24, 24, 0)
    edge_spread = as_ones(tap == lax.rem(place, 3) + jnp.where(at >= 48, 35, 0))
    at = lax.broadcasted_iota(jnp.int32, (rows, 96), 1)
    at = at - jnp.where(at >= 48, 48, 0)
    kinds = jnp.where(at >= 24, 1, 0)
    at = at - 24 * kinds
    edge_same = (lax.broadcasted_iota(jnp.int32, (rows, 96), 0) >> 5) == lax.div(at, 3)
    warp = warp_ref[...]
    for kind, matrix in enumerate((warp, squared(warp))):
        main_ref[kind] = jnp.where(same, dot(matrix, spread), 0.0).astype(BF16)
        kept = edge_same & (kinds == kind)
        edge_ref[kind] = jnp.where(kept, dot(matrix, edge_spread), 0.0).astype(BF16)
    source = lax.broadcasted_iota(jnp.int32, (TILE, TILE), 0)
    target = lax.broadcasted_iota(jnp.int32, (TILE, TILE), 1)
    near = jnp.abs(source - target) < 64
    for c in range(bands_ref.shape[0]):
        for b in range(3):
            row = jnp.broadcast_to(taps_ref[3 * c + b : 3 * c + b + 1], (TILE, TILE))
            turned = pltpu.roll(row, 0, 1, stride=1, stride_axis=0)
            cols = slice(b * TILE, (b + 1) * TILE)
            bands_ref[c, 0:TILE, cols] = jnp.where(near, turned, 0.0).astype(BF16)
            bands_ref[c, TILE : 2 * TILE, cols] = jnp.where(near, 0.0, turned).astype(BF16)


def selects_kernel(
    position_ref, send_patch, send_offset, request_patch, request_offset, *select_refs
):
    position = position_ref[0]
    for j in range(2):
        sums_refs = select_refs[4 * j : 4 * j + 4]
        keys = patch_keys((512, TILE), 0, (2, 1, 3, 0), j == 0, False, position)
        for source in range(4):
            hit = None
            for k in range(2):
                key = ccd_keys((1, TILE), 1, source, k, send_patch, send_offset)
                hit = keys == key if hit is None else hit | (keys == key)
            block = as_ones(hit)
            cols = slice(source * TILE, (source + 1) * TILE)
            for q, ref in enumerate(sums_refs):
                ref[:, cols] = block[q * TILE : (q + 1) * TILE]
    for j in range(2):
        own_ref, lent_ref = select_refs[8 + 2 * j : 10 + 2 * j]
        keys = patch_keys((1, 512), 1, (0, 1, 3, 2), j == 0, True, position)
        for source in range(4):
            key = ccd_keys((TILE, TILE), 0, source, j, request_patch, request_offset)
            out_ref = (own_ref, lent_ref)[source // 2]
            place = slice(source % 2 * TILE, (source % 2 + 1) * TILE)
            for q in range(4):
                cols = slice(q * TILE, (q + 1) * TILE)
                out_ref[place, cols] = as_ones(key == keys[:, cols])


def matrices(position, choices, row_warp, kernels):
    count, rows, reach = row_warp.shape
    flat = count * rows
    taps = kernels.shape[-1]
    turned = kernels.astype(F32).reshape(count * 3, taps)[:, ::-1]
    reachout = taps // 2
    turned = jnp.concatenate(
        [
            turned[:, reachout:],
            jnp.zeros((count * 3, TILE - taps), F32),
            turned[:, :reachout],
        ],
        axis=1,
    )
    smem = pl.BlockSpec(memory_space=pltpu.SMEM)
    vmem = pl.BlockSpec(memory_space=pltpu.VMEM)
    shapes = [(2, flat, flat), (2, flat, 96), (count, 256, 3 * TILE)]
    shapes += [(TILE, 4 * TILE)] * 8 + [(2 * TILE, 4 * TILE)] * 4

    def kernel(*refs):
        matrices_kernel(*refs[5:10])
        selects_kernel(*refs[:5], *refs[10:])

    return pl.pallas_call(
        kernel,
        out_shape=[jax.ShapeDtypeStruct(shape, BF16) for shape in shapes],
        in_specs=[smem] * 5 + [vmem] * 2,
        out_specs=[vmem] * len(shapes),
        compiler_params=pltpu.CompilerParams(vmem_limit_bytes=8 * MIB),
        cost_estimate=HINT,
    )(position.reshape(1), *choices, row_warp.reshape(flat, reach), turned)


def body(
    images,
    variances,
    row_warp,
    col_warp,
    warp_index,
    psf_kernels,
    psf_coeff,
    send_patch,
    send_offset,
    request_patch,
    request_offset,
    new_images,
):
    count, rows, columns = images.shape
    flat = count * rows
    blocks = list(zip(BOUNDS, BOUNDS[1:]))
    position = lax.axis_index("ccd")

    plain = images.reshape(flat, columns), variances.reshape(flat, columns)
    psf_coeff = psf_coeff.reshape(count, 3, columns // TILE, TILE)
    plain, col_warp, psf_coeff = jax.tree.map(in_hbm, (plain, col_warp, psf_coeff))
    tails, heads = strip_ends(*plain)
    before = strip_shift(tails, 1, wrap=False)
    after = strip_shift(heads, -1, wrap=False)
    choices = send_patch, send_offset, request_patch, request_offset
    main, edge, bands, *selects = matrices(position, choices, row_warp, psf_kernels)
    axes = [("x", "y"), ("y", "x")]

    steps = range(len(blocks))
    queue = [[main]]

    def ordered(function, *operands):
        result = function(*operands, queue[-1])
        queue.append([result[0]] if isinstance(result, (list, tuple)) else [result])
        return result

    def warped(part):
        low, high = ordered(
            ccd_block,
            part[0],
            part[1] - part[0],
            warp_index[:, 0],
            main,
            edge,
            bands,
            *plain,
            before,
            after,
            col_warp,
            psf_coeff,
        )
        return low, high, strip_shift(low, -1), strip_shift(high, 1)

    def started(j, source):
        two, one, three, _ = selects[4 * j : 4 * j + 4]
        up, down = ordered(first_sums, (two, one, three), source)
        return plane_shift(up, axes[j][0], 1), plane_shift(down, axes[j][0], -1)

    def rest(j, source):
        return ordered(second_sums, selects[4 * j + 1 : 4 * j + 4], source)

    sources = [warped(block) for block in blocks]
    sums, second = [], []
    for j in steps:
        sums.append(started(j, sources[j]))
        second.append(rest(j, sources[j]))
    passed = []
    for j in steps:
        up, down = ordered(passing_sums, *second[j][:2], *sums[j])
        passed.append((plane_shift(up, axes[j][0], 1), plane_shift(down, axes[j][0], -1)))
    spread = []
    for j in steps:
        axis = axes[j][1]
        kept, one, two, three = ordered(own_sums, second[j][2], *sums[j], *passed[j])
        two, one, three = [
            plane_shift(value, axis, shift) for value, shift in ((two, 2), (one, 1), (three, -1))
        ]
        spread.append((kept, (one, two, three)))
    left, rest_columns = ordered(coadded, *spread[0], columns // 2)
    coadds = left, ordered(later_coadded, *spread[1], rest_columns)
    pairs = [(coadd, plane_swap(coadd, axis, 1)) for (_, axis), coadd in zip(axes, coadds)]
    pairs = ordered(joined, pairs)
    pairs = [(pair, plane_swap(pair, axis, 3)) for (_, axis), pair in zip(axes, pairs)]
    held = []
    for (axis, _), block in zip(axes, ordered(joined, pairs)):
        held.append((block, plane_shift(block, axis, -1), plane_shift(block, axis, 1)))
    gathered = {}
    for j in steps:
        axis = axes[j][0]
        block, following, last = held[j]
        half = block.shape[1] // 2
        left = plane_shift(last[:, :half], axis, 1)
        right = plane_shift(following[:, half:], axis, -1)
        gathered[j] = block, following, last, left, right
    lent = {}
    for j in steps:
        own_select, lent_select = selects[8 + 2 * j : 10 + 2 * j]
        down, up = ordered(lent_rows, lent_select, gathered[j])
        lent[j] = own_select, strip_shift(down, 1), strip_shift(up, -1)
    results = None
    for j in steps:
        own_select, down, up = lent[j]
        first = j * columns // 2
        results = difference_block(first, own_select, gathered[j], new_images, down, up, results)
    difference, patch_coadd = results

    return (patch_coadd[None], difference)


def solution(mesh):
    return jax.shard_map(
        body,
        mesh=mesh,
        in_specs=(
            P("ccd", "strip", None),
            P("ccd", "strip", None),
            P("ccd", "strip", None),
            P(),
            P("ccd", "strip"),
            P("ccd", None, None),
            P("ccd", "strip", None, None),
            P("ccd", None),
            P("ccd", None),
            P("ccd", None),
            P("ccd", None),
            P("ccd", "strip", None),
        ),
        out_specs=(P("ccd", "strip", None), P("ccd", "strip", None)),
        check_vma=False,
    )
```

```python
import functools

import jax
import jax.numpy as jnp
from jax import lax
from jax.experimental import pallas as pl
from jax.experimental.pallas import tpu as pltpu
from jax.sharding import PartitionSpec as P

TILE = 128
SIDE = 4
HALF = 16
BOUNDS = (0, 2304, 4096)
F32 = jnp.float32
BF16 = jnp.bfloat16
MIB = 1024 * 1024


def strip_shift(value, steps, wrap=True):
    count = lax.axis_size("strip")
    pairs = [(i, (i + steps) % count) for i in range(count) if wrap or 0 <= i + steps < count]
    return lax.ppermute(value, "strip", pairs)


def plane_shift(value, axis, steps):
    pairs = []
    for i in range(SIDE * SIDE):
        y, x = divmod(i, SIDE)
        if axis == "x":
            x = (x + steps) % SIDE
        else:
            y = (y + steps) % SIDE
        pairs.append((i, y * SIDE + x))
    return lax.ppermute(value, "ccd", pairs)


def plane_swap(value, axis, mask):
    pairs = []
    for i in range(SIDE * SIDE):
        y, x = divmod(i, SIDE)
        pairs.append((i, y * SIDE + (x ^ mask) if axis == "x" else (y ^ mask) * SIDE + x))
    return lax.ppermute(value, "ccd", pairs)


def dot(a, b):
    return jnp.dot(a, b, preferred_element_type=F32)


def in_hbm(value):
    return pltpu.with_memory_space_constraint(value, pltpu.HBM)


def squared(values):
    wide = values.astype(F32)
    return (wide * wide).astype(BF16)


HINT = pl.CostEstimate(flops=1, bytes_accessed=1, transcendentals=0)


def vmem_call(kernel, shapes, operands, ahead=()):
    count = len(operands)

    def ordered(*refs):
        kernel(*refs[:count], *refs[count + len(ahead) :])

    vmem = pl.BlockSpec(memory_space=pltpu.VMEM)
    return pl.pallas_call(
        ordered,
        out_shape=[jax.ShapeDtypeStruct(shape, dtype) for shape, dtype in shapes],
        in_specs=[vmem] * count + [pl.BlockSpec(memory_space=pl.ANY)] * len(ahead),
        out_specs=[vmem] * len(shapes),
        compiler_params=pltpu.CompilerParams(vmem_limit_bytes=16 * MIB),
        cost_estimate=HINT,
    )(*operands, *ahead)


def ccd_kernel(
    first,
    width,
    columns,
    pick_ref,
    main_ref,
    edge_ref,
    bands_ref,
    images_hbm,
    variances_hbm,
    before_hbm,
    after_hbm,
    table_hbm,
    coeff_hbm,
    ahead_ref,
    low_ref,
    high_ref,
    pixels,
    rims,
    table,
    coeff,
    rowed,
    warped,
    inverse,
    sems,
):
    tiles = width // TILE
    all_tiles = columns // TILE
    t0 = first // TILE
    start = max(first - 2 * TILE, 0)
    stop = min(first + width + 2 * TILE, columns)
    span = stop - start
    table_start = max(t0 - 1, 0)
    table_stop = min(t0 + tiles + 1, all_tiles)
    rows = main_ref.shape[1]
    ccds = rows // 32
    edge_rows = before_hbm.shape[0]
    pieces = [(0, 768), (768, span - 768)]
    loads = []
    for p, (at, size) in enumerate(pieces):
        here, there = pl.ds(at, size), pl.ds(start + at, size)
        loads.append(
            [
                pltpu.make_async_copy(
                    images_hbm.at[:, there], pixels.at[0, :, here], sems.at[4 * p]
                ),
                pltpu.make_async_copy(
                    variances_hbm.at[:, there], pixels.at[1, :, here], sems.at[4 * p + 1]
                ),
                pltpu.make_async_copy(
                    before_hbm.at[:, there], rims.at[pl.ds(0, edge_rows), here], sems.at[4 * p + 2]
                ),
                pltpu.make_async_copy(
                    after_hbm.at[:, there],
                    rims.at[pl.ds(edge_rows, edge_rows), here],
                    sems.at[4 * p + 3],
                ),
            ]
        )
    load_table = pltpu.make_async_copy(
        table_hbm.at[:, pl.ds(table_start, table_stop - table_start), pl.ds(64, 256), :],
        table,
        sems.at[8],
    )
    load_coeff = pltpu.make_async_copy(
        coeff_hbm, coeff, sems.at[9]
    )
    for copy in loads[0] + loads[1] + [load_table, load_coeff]:
        copy.start()
    shift = (start - (first - 2 * TILE)) // TILE
    if shift > 0:
        rowed[:, 0:shift] = jnp.zeros((2, shift, rows, TILE), BF16)
    end = shift + span // TILE
    if end < tiles + 4:
        rowed[:, end : tiles + 4] = jnp.zeros((2, tiles + 4 - end, rows, TILE), BF16)
    for (at, size), copies in zip(pieces, loads):
        for copy in copies:
            copy.wait()
        for j in range(at // 256, (at + size) // 256):
            here = slice(j * 256, (j + 1) * 256)
            edges = rims[:, here]
            for kind in range(2):
                out = dot(main_ref[kind], pixels[kind, :, here]) + dot(edge_ref[kind], edges)
                out = out.astype(BF16)
                rowed[kind, shift + 2 * j] = out[:, :TILE]
                rowed[kind, shift + 2 * j + 1] = out[:, TILE:]
    load_table.wait()
    lane = lax.broadcasted_iota(jnp.int32, (rows, TILE), 1)

    def with_halo(own, previous, following):
        halo = jnp.where(lane[: own.shape[0]] < 64, following, previous)
        return jnp.concatenate([own, halo], axis=1)

    def weights(k):
        parts = []
        for m in range(2):
            part = table[m, k]
            parts.append(jnp.concatenate([part[64:192], part[192:256], part[0:64]], axis=0))
        return jnp.concatenate(parts, axis=1)

    def choose(product, c):
        block = product[c * 32 : (c + 1) * 32]
        return jnp.where(pick_ref[c] == 0, block[:, :TILE], block[:, TILE:])

    def column_step(w, with_variance):
        matrix = weights(w + (t0 - 1 - table_start))
        product = dot(with_halo(rowed[0, w + 1], rowed[0, w], rowed[0, w + 2]), matrix)
        at = pl.ds(pl.multiple_of(w * 32, 32), 32)
        for c in range(ccds):
            warped[c, at] = choose(product, c).astype(BF16)
        if with_variance:
            product = dot(
                with_halo(rowed[1, w + 1], rowed[1, w], rowed[1, w + 2]), squared(matrix)
            )
            at = pl.ds(pl.multiple_of((w - 1) * 32, 32), 32)
            for c in range(ccds):
                inverse[c, at] = 1.0 / choose(product, c)

    for w in (0, tiles + 1):
        if 0 <= t0 - 1 + w < all_tiles:
            column_step(w, False)
        else:
            warped[:, w * 32 : (w + 1) * 32] = jnp.zeros((ccds, 32, TILE), BF16)

    group = max(size for size in range(1, 9) if tiles % size == 0)

    def column_loop(w, carry):
        column_step(w, True)
        return carry

    lax.fori_loop(1, tiles + 1, column_loop, 0, unroll=tiles)
    load_coeff.wait()

    def ccd_step(c, carry):
        row16 = pl.ds(pl.multiple_of(c * HALF, HALF), HALF)
        for g in range(tiles // group):
            base = g * group * 32
            size = group * 32
            own = warped[c, base + 32 : base + 32 + size]
            lhs = with_halo(
                own, warped[c, base : base + size], warped[c, base + 64 : base + 64 + size]
            )
            convolved = dot(lhs, bands_ref[c])
            for k in range(group):
                tile = g * group + k
                here = slice(k * 32, (k + 1) * 32)
                matched = own[here].astype(F32)
                for b in range(3):
                    factor = coeff[c, b, t0 + tile : t0 + tile + 1]
                    matched = matched + factor * convolved[here, b * TILE : (b + 1) * TILE]
                weight = inverse[c, tile * 32 : (tile + 1) * 32]
                flux = (matched * weight).astype(BF16)
                weight = weight.astype(BF16)
                left = slice(tile * TILE, (tile + 1) * TILE)
                right = slice(width + tile * TILE, width + (tile + 1) * TILE)
                low_ref[row16, left] = flux[:HALF]
                high_ref[row16, left] = flux[HALF:]
                low_ref[row16, right] = weight[:HALF]
                high_ref[row16, right] = weight[HALF:]
        return carry

    lax.fori_loop(0, ccds, ccd_step, 0, unroll=ccds)


def ccd_block(
    first, width, pick, main, edge, bands, images, variances, before, after, col_warp, coeff, ahead
):
    rows, columns = images.shape
    tiles = width // TILE
    span = min(first + width + 2 * TILE, columns) - max(first - 2 * TILE, 0)
    table_tiles = min(first // TILE + tiles + 1, columns // TILE) - max(first // TILE - 1, 0)
    ccds = rows // 32
    vmem = pl.BlockSpec(memory_space=pltpu.VMEM)
    anywhere = pl.BlockSpec(memory_space=pl.ANY)
    hbm = pl.BlockSpec(memory_space=pltpu.HBM)
    out = jax.ShapeDtypeStruct((rows // 2, 2 * width), BF16)
    return pl.pallas_call(
        functools.partial(ccd_kernel, first, width, columns),
        out_shape=(out, out),
        in_specs=[pl.BlockSpec(memory_space=pltpu.SMEM)] + [vmem] * 3 + [hbm] * 2 + [anywhere] * 2 + [hbm] * 2 + [anywhere],
        out_specs=(vmem, vmem),
        scratch_shapes=[
            pltpu.VMEM((2, rows, span), BF16),
            pltpu.VMEM((2 * before.shape[0], span), BF16),
            pltpu.VMEM((2, table_tiles, 256, TILE), BF16),
            pltpu.VMEM(coeff.shape, F32),
            pltpu.VMEM((2, tiles + 4, rows, TILE), BF16),
            pltpu.VMEM((ccds, (tiles + 2) * 32, TILE), BF16),
            pltpu.VMEM((ccds, tiles * 32, TILE), F32),
            pltpu.SemaphoreType.DMA((10,)),
        ],
        compiler_params=pltpu.CompilerParams(vmem_limit_bytes=24 * MIB),
        cost_estimate=HINT,
    )(pick, main, edge, bands, images, variances, before, after, col_warp, coeff, ahead[0])


def ends_kernel(images_hbm, variances_hbm, tails_ref, heads_ref, pixels, sems):
    _, rows, columns = pixels.shape
    step = columns // 4
    copies = []
    for p in range(4):
        cols = pl.ds(p * step, step)
        for kind, source in enumerate((images_hbm, variances_hbm)):
            copies.append(
                pltpu.make_async_copy(
                    source.at[:, cols], pixels.at[kind, :, cols], sems.at[2 * p + kind]
                )
            )
    for copy in copies:
        copy.start()
    for p in range(4):
        for kind in range(2):
            copies[2 * p + kind].wait()
        for low in range(p * step, (p + 1) * step, 256):
            cols = slice(low, low + 256)
            tails, heads = [], []
            for kind in range(2):
                for c in range(rows // 32):
                    tail = pixels[kind, c * 32 + 16 : c * 32 + 32, cols].astype(F32)
                    tails.append(tail[13:])
                    heads.append(pixels[kind, c * 32 : c * 32 + 16, cols].astype(F32)[:3])
            tails_ref[:, cols] = jnp.concatenate(tails, axis=0).astype(BF16)
            heads_ref[:, cols] = jnp.concatenate(heads, axis=0).astype(BF16)


def strip_ends(images, variances):
    rows, columns = images.shape
    out = jax.ShapeDtypeStruct((48, columns), BF16)
    vmem = pl.BlockSpec(memory_space=pltpu.VMEM)
    return pl.pallas_call(
        ends_kernel,
        out_shape=(out, out),
        in_specs=[pl.BlockSpec(memory_space=pltpu.HBM)] * 2,
        out_specs=(vmem, vmem),
        scratch_shapes=[pltpu.VMEM((2, rows, columns), BF16), pltpu.SemaphoreType.DMA((8,))],
        compiler_params=pltpu.CompilerParams(vmem_limit_bytes=8 * MIB),
        cost_estimate=HINT,
    )(images, variances)


def pieces_of(width, cuts=(), step=512):
    edges = sorted({0, width, *(cut for cut in cuts if 0 < cut < width)})
    pieces = []
    for low, high in zip(edges, edges[1:]):
        pieces += [(at, min(at + step, high)) for at in range(low, high, step)]
    return pieces


def stacked(refs, cols):
    return jnp.concatenate([ref[:, cols] for ref in refs], axis=0)


def first_kernel(two_ref, one_ref, three_ref, *refs):
    up_ref, down_ref = refs[4:]
    width = up_ref.shape[1]
    half = two_ref.shape[0]
    for side_ref, base in ((three_ref, 0), (one_ref, width)):
        select = jnp.concatenate([two_ref[...], side_ref[...]], axis=0)
        for low, high in pieces_of(width):
            out = dot(select, stacked(refs[:4], slice(base + low, base + high))).astype(BF16)
            if base == 0:
                up_ref[:half, low:high] = out[:half]
                down_ref[half:, low:high] = out[half:]
            else:
                down_ref[:half, low:high] = out[:half]
                up_ref[half:, low:high] = out[half:]


def second_kernel(one_ref, three_ref, own_select_ref, *refs):
    up_ref, down_ref, own_ref = refs[4:]
    width = up_ref.shape[1]
    half = one_ref.shape[0]
    for side_ref, base, out_ref in ((one_ref, 0, up_ref), (three_ref, width, down_ref)):
        select = jnp.concatenate([side_ref[...], own_select_ref[...]], axis=0)
        for low, high in pieces_of(width):
            out = dot(select, stacked(refs[:4], slice(base + low, base + high))).astype(BF16)
            out_ref[:, low:high] = out[:half]
            own_ref[:, base + low : base + high] = out[half:]


def first_sums(selects, sources, ahead):
    shape = (2 * selects[0].shape[0], sources[0].shape[1] // 2)
    return vmem_call(first_kernel, [(shape, BF16)] * 2, [*selects, *sources], ahead)


def second_sums(selects, sources, ahead):
    rows, width = selects[0].shape[0], sources[0].shape[1]
    shapes = [(rows, width // 2), (rows, width // 2), (rows, width)]
    shapes = [(shape, BF16) for shape in shapes]
    return vmem_call(second_kernel, shapes, [*selects, *sources], ahead)


def total(*terms):
    result = terms[0].astype(F32)
    for term in terms[1:]:
        result = result + term.astype(F32)
    return result


def passing_kernel(up_ref, down_ref, last_ref, next_ref, up_out, down_out):
    rows, width = up_ref.shape
    for low, high in pieces_of(width, step=256):
        cols = slice(low, high)
        up_out[:, cols] = total(up_ref[:, cols], last_ref[:rows, cols]).astype(BF16)
        down_out[:, cols] = total(down_ref[:, cols], next_ref[:rows, cols]).astype(BF16)


def passing_sums(up, down, from_last, from_next, ahead):
    shapes = [(up.shape, BF16), (down.shape, BF16)]
    return vmem_call(passing_kernel, shapes, [up, down, from_last, from_next], ahead)


def own_kernel(own_ref, last_ref, next_ref, flux_ref, weight_ref, kept_ref, *rest_refs):
    rows, width = flux_ref.shape
    strip = kept_ref.shape[0]
    for low, high in pieces_of(width, step=256):
        cols, right = slice(low, high), slice(width + low, width + high)
        flux = total(own_ref[:, cols], next_ref[rows:, cols], flux_ref[:, cols])
        weight = total(own_ref[:, right], last_ref[rows:, cols], weight_ref[:, cols])
        for at, values in ((cols, flux), (right, weight)):
            kept_ref[:, at] = values[:strip]
            for k, rest_ref in enumerate(rest_refs):
                rest_ref[:, at] = values[(k + 1) * strip : (k + 2) * strip].astype(BF16)


def own_sums(own, from_last, from_next, flux, weight, ahead):
    shape = (own.shape[0] // SIDE, own.shape[1])
    shapes = [(shape, F32)] + [(shape, BF16)] * 3
    return vmem_call(own_kernel, shapes, [own, from_last, from_next, flux, weight], ahead)


def coadd_kernel(*refs):
    terms, (left_ref, rest_ref) = refs[:4], refs[4:]
    width, middle = terms[0].shape[1] // 2, left_ref.shape[1]
    for low, high in pieces_of(width, (middle,), step=256):
        numerator = total(*[ref[:, low:high] for ref in terms])
        denominator = total(*[ref[:, width + low : width + high] for ref in terms])
        result = (numerator / (1.0 + denominator)).astype(BF16)
        if high <= middle:
            left_ref[:, low:high] = result
        else:
            rest_ref[:, low - middle : high - middle] = result


def later_coadd_kernel(*refs):
    terms, (rest_ref, right_ref) = refs[:4], refs[4:]
    width, base = terms[0].shape[1] // 2, rest_ref.shape[1]
    right_ref[:, :base] = rest_ref[...]
    for low, high in pieces_of(width, step=256):
        numerator = total(*[ref[:, low:high] for ref in terms])
        denominator = total(*[ref[:, width + low : width + high] for ref in terms])
        right_ref[:, base + low : base + high] = (numerator / (1.0 + denominator)).astype(BF16)


def coadded(kept, arrived, half, ahead):
    rows = kept.shape[0]
    shapes = [((rows, half), BF16), ((rows, kept.shape[1] // 2 - half), BF16)]
    return vmem_call(coadd_kernel, shapes, [kept, *arrived], ahead)


def later_coadded(kept, arrived, rest, ahead):
    shape = (kept.shape[0], kept.shape[1] // 2 + rest.shape[1])
    return vmem_call(later_coadd_kernel, [(shape, BF16)], [kept, *arrived, rest], ahead)[0]


def join_kernel(*refs):
    count = len(refs) // 3
    for first_ref, second_ref, out_ref in zip(refs[::2], refs[1::2], refs[2 * count :]):
        rows = first_ref.shape[0]
        out_ref[:rows] = first_ref[...]
        out_ref[rows:] = second_ref[...]


def joined(pairs, ahead):
    shapes = [((2 * first.shape[0], first.shape[1]), BF16) for first, _ in pairs]
    return vmem_call(join_kernel, shapes, [value for pair in pairs for value in pair], ahead)


def patch_pieces(patch_refs):
    own_ref, next_ref, last_ref, left_ref, right_ref = patch_refs
    width, half = own_ref.shape[1], left_ref.shape[1]
    for low, high in pieces_of(width, (half,)):
        far_ref, base = (left_ref, 0) if high <= half else (right_ref, half)
        cols = slice(low, high)
        stack = [ref[:, cols] for ref in (own_ref, next_ref, last_ref)]
        stack.append(far_ref[:, low - base : high - base])
        yield low, high, jnp.concatenate(stack, axis=0)


def lend_kernel(select_ref, *refs):
    down_ref, up_ref = refs[5:]
    half = up_ref.shape[0] - HALF
    for ref in (down_ref, up_ref):
        ref[half:] = refs[0][HALF : 2 * HALF]
    for low, high, stack in patch_pieces(refs[:5]):
        out = dot(select_ref[...], stack).astype(BF16)
        down_ref[:half, low:high] = out[:half]
        up_ref[:half, low:high] = out[half:]


def lent_rows(select, patches, ahead):
    rows, width = select.shape[0] // 2, patches[0].shape[1]
    shapes = [((rows + HALF, width), BF16)] * 2
    return vmem_call(lend_kernel, shapes, [select, *patches], ahead)


def template_kernel(select_ref, *refs):
    for low, high, stack in patch_pieces(refs[:5]):
        refs[5][:, low:high] = dot(select_ref[...], stack).astype(BF16)


def own_template(select, patches, ahead):
    shape = (select.shape[0], patches[0].shape[1])
    return vmem_call(template_kernel, [(shape, BF16)], [select, *patches], ahead)[0]


def difference_kernel(first, template_ref, coadd_ref, new_hbm, down_ref, up_ref, *refs):
    out_hbm, coadd_hbm, new, result, coadd, sems = refs[-6:]
    count, _, width = new.shape
    here = pl.ds(first, width)
    coadd[:HALF] = down_ref[count * HALF :]
    coadd[HALF:] = coadd_ref[:HALF]
    store_coadd = pltpu.make_async_copy(coadd, coadd_hbm.at[:, here], sems.at[1])
    store_coadd.start()
    load = pltpu.make_async_copy(new_hbm.at[:, :, here], new, sems.at[0])
    load.start()
    stores = [store_coadd]
    for p, (low, high) in enumerate(pieces_of(width)):
        cols = slice(low, high)
        own = template_ref[:, cols].astype(F32)
        if p == 0:
            load.wait()
        for c in range(count):
            here = slice(c * HALF, (c + 1) * HALF)
            there = slice((count + c) * HALF, (count + c + 1) * HALF)
            lower = own[here] + down_ref[here, cols].astype(F32)
            upper = own[there] + up_ref[here, cols].astype(F32)
            result[c, 0:HALF, cols] = (new[c, 0:HALF, cols].astype(F32) - lower).astype(BF16)
            result[c, HALF : 2 * HALF, cols] = (
                new[c, HALF : 2 * HALF, cols].astype(F32) - upper
            ).astype(BF16)
        store = pltpu.make_async_copy(
            result.at[:, :, pl.ds(low, high - low)],
            out_hbm.at[:, :, pl.ds(first + low, high - low)],
            sems.at[2 + p],
        )
        store.start()
        stores.append(store)
    for store in stores:
        store.wait()


def difference_block(first, template, coadd, new_images, down, up, running):
    width = template.shape[1]
    count, strip_rows, columns = new_images.shape
    vmem = pl.BlockSpec(memory_space=pltpu.VMEM)
    hbm = pl.BlockSpec(memory_space=pltpu.HBM)
    operands = [template, coadd, new_images, down, up]
    specs = [vmem] * 2 + [pl.BlockSpec(memory_space=pl.ANY)] + [vmem] * 2
    aliases = {}
    if running is not None:
        aliases = {len(operands): 0, len(operands) + 1: 1}
        operands += running
        specs += [hbm, hbm]
    count_pieces = len(pieces_of(width))
    block = pltpu.VMEM((count, strip_rows, width), BF16)
    return pl.pallas_call(
        functools.partial(difference_kernel, first),
        out_shape=[
            jax.ShapeDtypeStruct(new_images.shape, BF16),
            jax.ShapeDtypeStruct((strip_rows, columns), BF16),
        ],
        in_specs=specs,
        out_specs=[hbm, hbm],
        scratch_shapes=[
            block,
            block,
            pltpu.VMEM((strip_rows, width), BF16),
            pltpu.SemaphoreType.DMA((2 + count_pieces,)),
        ],
        input_output_aliases=aliases,
        compiler_params=pltpu.CompilerParams(vmem_limit_bytes=16 * MIB),
        cost_estimate=HINT,
    )(*operands)


def ring_step(index, table):
    value = jnp.full_like(index, table[3])
    for k in range(3):
        value = jnp.where(index == k, table[k], value)
    return value


def patch_keys(shape, axis, table, x_first, swapped, position):
    at = lax.broadcasted_iota(jnp.int32, shape, axis)
    outer, inner = ring_step(at >> 7, table), (at >> 5) & 3
    base = position >> 2, position & 3
    outer_base, inner_base = base[::-1] if x_first else base
    outer = (outer_base + outer) & 3
    inner = inner_base ^ inner ^ (inner >> 1) if swapped else (inner_base + inner) & 3
    y, x = (inner, outer) if x_first else (outer, inner)
    name = (y << 2) + x
    return (name << 8) + HALF + (at & 31)


def ccd_keys(shape, axis, source, k, patch_ref, offset_ref):
    at = lax.broadcasted_iota(jnp.int32, shape, axis)
    ccd, row = at >> 4, at & 15
    key = row + (0, HALF, 2 * HALF, -HALF)[source]
    for c in range(8):
        known = (patch_ref[c, k] << 8) + offset_ref[c, k]
        key = key + jnp.where(ccd == c, known, 0)
    return key


def as_ones(mask):
    return jnp.where(mask, 1.0, 0.0).astype(BF16)


def matrices_kernel(warp_ref, taps_ref, main_ref, edge_ref, bands_ref):
    rows, reach = warp_ref.shape
    at = lax.broadcasted_iota(jnp.int32, (reach, rows), 1)
    tap = lax.broadcasted_iota(jnp.int32, (reach, rows), 0)
    spread = as_ones(tap == (at & 31) + 3)
    own = lax.broadcasted_iota(jnp.int32, (rows, rows), 0) >> 5
    same = own == lax.broadcasted_iota(jnp.int32, (rows, rows), 1) >> 5
    at = lax.broadcasted_iota(jnp.int32, (reach, 96), 1)
    tap = lax.broadcasted_iota(jnp.int32, (reach, 96), 0)
    place = at - jnp.where(at >= 48, 48, 0)
    place = place - jnp.where(place >= 24, 24, 0)
    edge_spread = as_ones(tap == lax.rem(place, 3) + jnp.where(at >= 48, 35, 0))
    at = lax.broadcasted_iota(jnp.int32, (rows, 96), 1)
    at = at - jnp.where(at >= 48, 48, 0)
    kinds = jnp.where(at >= 24, 1, 0)
    at = at - 24 * kinds
    edge_same = (lax.broadcasted_iota(jnp.int32, (rows, 96), 0) >> 5) == lax.div(at, 3)
    warp = warp_ref[...]
    for kind, matrix in enumerate((warp, squared(warp))):
        main_ref[kind] = jnp.where(same, dot(matrix, spread), 0.0).astype(BF16)
        kept = edge_same & (kinds == kind)
        edge_ref[kind] = jnp.where(kept, dot(matrix, edge_spread), 0.0).astype(BF16)
    source = lax.broadcasted_iota(jnp.int32, (TILE, TILE), 0)
    target = lax.broadcasted_iota(jnp.int32, (TILE, TILE), 1)
    near = jnp.abs(source - target) < 64
    for c in range(bands_ref.shape[0]):
        for b in range(3):
            row = jnp.broadcast_to(taps_ref[3 * c + b : 3 * c + b + 1], (TILE, TILE))
            turned = pltpu.roll(row, 0, 1, stride=1, stride_axis=0)
            cols = slice(b * TILE, (b + 1) * TILE)
            bands_ref[c, 0:TILE, cols] = jnp.where(near, turned, 0.0).astype(BF16)
            bands_ref[c, TILE : 2 * TILE, cols] = jnp.where(near, 0.0, turned).astype(BF16)


def selects_kernel(
    position_ref, send_patch, send_offset, request_patch, request_offset, *select_refs
):
    position = position_ref[0]
    for j in range(2):
        sums_refs = select_refs[4 * j : 4 * j + 4]
        keys = patch_keys((512, TILE), 0, (2, 1, 3, 0), j == 0, False, position)
        for source in range(4):
            hit = None
            for k in range(2):
                key = ccd_keys((1, TILE), 1, source, k, send_patch, send_offset)
                hit = keys == key if hit is None else hit | (keys == key)
            block = as_ones(hit)
            cols = slice(source * TILE, (source + 1) * TILE)
            for q, ref in enumerate(sums_refs):
                ref[:, cols] = block[q * TILE : (q + 1) * TILE]
    for j in range(2):
        own_ref, lent_ref = select_refs[8 + 2 * j : 10 + 2 * j]
        keys = patch_keys((1, 512), 1, (0, 1, 3, 2), j == 0, True, position)
        for source in range(4):
            key = ccd_keys((TILE, TILE), 0, source, j, request_patch, request_offset)
            out_ref = (own_ref, lent_ref)[source // 2]
            place = slice(source % 2 * TILE, (source % 2 + 1) * TILE)
            for q in range(4):
                cols = slice(q * TILE, (q + 1) * TILE)
                out_ref[place, cols] = as_ones(key == keys[:, cols])


def matrices(position, choices, row_warp, kernels):
    count, rows, reach = row_warp.shape
    flat = count * rows
    taps = kernels.shape[-1]
    turned = kernels.astype(F32).reshape(count * 3, taps)[:, ::-1]
    reachout = taps // 2
    turned = jnp.concatenate(
        [
            turned[:, reachout:],
            jnp.zeros((count * 3, TILE - taps), F32),
            turned[:, :reachout],
        ],
        axis=1,
    )
    smem = pl.BlockSpec(memory_space=pltpu.SMEM)
    vmem = pl.BlockSpec(memory_space=pltpu.VMEM)
    shapes = [(2, flat, flat), (2, flat, 96), (count, 256, 3 * TILE)]
    shapes += [(TILE, 4 * TILE)] * 8 + [(2 * TILE, 4 * TILE)] * 4

    def kernel(*refs):
        matrices_kernel(*refs[5:10])
        selects_kernel(*refs[:5], *refs[10:])

    return pl.pallas_call(
        kernel,
        out_shape=[jax.ShapeDtypeStruct(shape, BF16) for shape in shapes],
        in_specs=[smem] * 5 + [vmem] * 2,
        out_specs=[vmem] * len(shapes),
        compiler_params=pltpu.CompilerParams(vmem_limit_bytes=8 * MIB),
        cost_estimate=HINT,
    )(position.reshape(1), *choices, row_warp.reshape(flat, reach), turned)


def body(
    images,
    variances,
    row_warp,
    col_warp,
    warp_index,
    psf_kernels,
    psf_coeff,
    send_patch,
    send_offset,
    request_patch,
    request_offset,
    new_images,
):
    count, rows, columns = images.shape
    flat = count * rows
    blocks = list(zip(BOUNDS, BOUNDS[1:]))
    position = lax.axis_index("ccd")

    plain = images.reshape(flat, columns), variances.reshape(flat, columns)
    psf_coeff = psf_coeff.reshape(count, 3, columns // TILE, TILE)
    plain, col_warp, psf_coeff = jax.tree.map(in_hbm, (plain, col_warp, psf_coeff))
    tails, heads = strip_ends(*plain)
    before = strip_shift(tails, 1, wrap=False)
    after = strip_shift(heads, -1, wrap=False)
    choices = send_patch, send_offset, request_patch, request_offset
    main, edge, bands, *selects = matrices(position, choices, row_warp, psf_kernels)
    axes = [("x", "y"), ("y", "x")]

    steps = range(len(blocks))
    queue = [[main]]

    def ordered(function, *operands):
        result = function(*operands, queue[-1])
        queue.append([result[0]] if isinstance(result, (list, tuple)) else [result])
        return result

    def warped(part):
        low, high = ordered(
            ccd_block,
            part[0],
            part[1] - part[0],
            warp_index[:, 0],
            main,
            edge,
            bands,
            *plain,
            before,
            after,
            col_warp,
            psf_coeff,
        )
        return low, high, strip_shift(low, -1), strip_shift(high, 1)

    def started(j, source):
        two, one, three, _ = selects[4 * j : 4 * j + 4]
        up, down = ordered(first_sums, (two, one, three), source)
        return plane_shift(up, axes[j][0], 1), plane_shift(down, axes[j][0], -1)

    def rest(j, source):
        return ordered(second_sums, selects[4 * j + 1 : 4 * j + 4], source)

    sources = [warped(block) for block in blocks]
    sums, second = [], []
    for j in steps:
        sums.append(started(j, sources[j]))
        second.append(rest(j, sources[j]))
    passed = []
    for j in steps:
        up, down = ordered(passing_sums, *second[j][:2], *sums[j])
        passed.append((plane_shift(up, axes[j][0], 1), plane_shift(down, axes[j][0], -1)))
    spread = []
    for j in steps:
        axis = axes[j][1]
        kept, one, two, three = ordered(own_sums, second[j][2], *sums[j], *passed[j])
        two, one, three = [
            plane_shift(value, axis, shift) for value, shift in ((two, 2), (one, 1), (three, -1))
        ]
        spread.append((kept, (one, two, three)))
    left, rest_columns = ordered(coadded, *spread[0], columns // 2)
    coadds = left, ordered(later_coadded, *spread[1], rest_columns)
    pairs = [(coadd, plane_swap(coadd, axis, 1)) for (_, axis), coadd in zip(axes, coadds)]
    pairs = ordered(joined, pairs)
    pairs = [(pair, plane_swap(pair, axis, 3)) for (_, axis), pair in zip(axes, pairs)]
    held = []
    for (axis, _), block in zip(axes, ordered(joined, pairs)):
        held.append((block, plane_shift(block, axis, -1), plane_shift(block, axis, 1)))
    gathered = {}
    for j in steps:
        axis = axes[j][0]
        block, following, last = held[j]
        half = block.shape[1] // 2
        left = plane_shift(last[:, :half], axis, 1)
        right = plane_shift(following[:, half:], axis, -1)
        gathered[j] = block, following, last, left, right
    lent = {}
    for j in steps:
        own_select, lent_select = selects[8 + 2 * j : 10 + 2 * j]
        down, up = ordered(lent_rows, lent_select, gathered[j])
        lent[j] = own_select, strip_shift(down, 1), strip_shift(up, -1)
    templates = [ordered(own_template, lent[j][0], gathered[j]) for j in steps]
    results = None
    for j in steps:
        _, down, up = lent[j]
        first = j * columns // 2
        results = difference_block(first, templates[j], coadds[j], new_images, down, up, results)
    difference, patch_coadd = results

    return (patch_coadd[None], difference)


def solution(mesh):
    return jax.shard_map(
        body,
        mesh=mesh,
        in_specs=(
            P("ccd", "strip", None),
            P("ccd", "strip", None),
            P("ccd", "strip", None),
            P(),
            P("ccd", "strip"),
            P("ccd", None, None),
            P("ccd", "strip", None, None),
            P("ccd", None),
            P("ccd", None),
            P("ccd", None),
            P("ccd", None),
            P("ccd", "strip", None),
        ),
        out_specs=(P("ccd", "strip", None), P("ccd", "strip", None)),
        check_vma=False,
    )
```
